256 devices in a mesh: lat: 64 (over z, x, y_lo), lev: 4 (over y_hi, core).
Axes of the slice: x: 4, y: 4 (y_hi: 2, y_lo: 2; y = y_hi * 2 + y_lo), z: 8, core: 2. Of those that a mesh axis runs over, the one named last changes fastest.
Arguments:
- tracers: float32 [8, 8, 768, 1152], P(None, 'lev', 'lat'), may hold values from -6 to 6
- courant_x: float32 [8, 768, 1152], P('lev', 'lat'), may hold values from -0.95 to 0.95
- courant_y: float32 [8, 768, 1152], P('lev', 'lat'), may hold values from -0.95 to 0.95
- thickness: float32 [8, 768, 1152], P('lev', 'lat'), may hold values from 0.5 to 1.5
- level_weights: float32 [8], replicated, may hold values from 0.5 to 2
- surface_geo: float32 [768, 1152], P('lat'), may hold values from -6 to 6
Outputs:
- remapped: float32 [8, 8, 768, 1152], P(None, 'lev', 'lat')
- geopotential: float32 [8, 768, 1152], P('lev', 'lat')
The draws below stay inside these ranges and needn't reach their ends.
All inputs are finite; a program needn't handle non-finite values.
Results may differ from the reference program's by a relative error of at most 0.0003.
Values sent between devices are 32-bit elements; how exact they have to be, the bound alone decides.
A program may use at most 64 MiB of HBM per device.

```python
import math
import jax
import jax.numpy as jnp
from jax import lax

NLON = 1152
FIELDS = 8
SUBSTEPS = 4
LAT = 768
NLEV = 8


def block_scale(rng, extent, shards, low, high):
    def one(dim, shards_of):
        draws = jax.random.uniform(jax.random.fold_in(jax.random.fold_in(rng, 6), dim), (shards_of,), jnp.float32, low / len(shards), high / len(shards))
        return jnp.repeat(jnp.exp(draws), extent[dim] // shards_of).reshape((-1,) + (1,) * (len(extent) - dim - 1))

    factor_of = one(*shards[0])
    for cut in shards[1:]:
        factor_of = factor_of * one(*cut)
    return factor_of


def gaussian(stream_key, dims, spread, reach, cuts=(), kind=jnp.bfloat16):
    drawn = jax.random.normal(stream_key, dims, jnp.float32) * spread
    if len(cuts) > 0:
        drawn = block_scale(stream_key, dims, cuts, -0.22, 0.18) * drawn
    return jnp.clip(drawn, min=-reach, max=reach).astype(kind)


def setup_inputs(seed: int = 0) -> dict:
    splits = jax.random.split(jax.random.key(seed), 7)
    tracers = gaussian(splits[0], (FIELDS, NLEV, LAT, NLON), 1.0, 6.0, ((1, 4), (2, 64)), jnp.float32)
    courant_x = jnp.clip(jax.random.uniform(splits[1], (NLEV, LAT, NLON), jnp.float32, -0.95, 0.95) * block_scale(splits[1], (NLEV, LAT, NLON), ((0, 4), (1, 64)), -0.4, 0.0), -0.95, 0.95)
    courant_y = jnp.clip(jax.random.uniform(splits[2], (NLEV, LAT, NLON), jnp.float32, -0.95, 0.95) * block_scale(splits[2], (NLEV, LAT, NLON), ((0, 4), (1, 64)), -0.4, 0.0), -0.95, 0.95)
    thickness = jnp.clip(0.5 + 1.0 * jax.random.uniform(splits[3], (NLEV, LAT, NLON), jnp.float32) ** block_scale(splits[3], (NLEV, LAT, NLON), ((0, 4), (1, 64)), -0.2, 0.2), 0.5, 1.5)
    level_weights = jnp.clip(jnp.exp(jax.random.uniform(splits[4], (NLEV,), jnp.float32, math.log(0.5), math.log(2.0))), 0.5, 2.0)
    surface_geo = gaussian(splits[5], (LAT, NLON), 1.0, 6.0, ((0, 64),), jnp.float32)
    return {"tracers": tracers, "courant_x": courant_x, "courant_y": courant_y, "thickness": thickness, "level_weights": level_weights, "surface_geo": surface_geo}


top_pressure = 1.0
gas_factor = 0.3


def ppm_flux(courant, left_pos, right_pos, mean_pos, left_neg, right_neg, mean_neg):
    slope = right_pos - left_pos
    curve = 6.0 * (mean_pos - 0.5 * (left_pos + right_pos))
    forward = courant * (right_pos - 0.5 * courant * (slope - (1.0 - 2.0 * courant / 3.0) * curve))
    upwind = -courant
    slope_neg = right_neg - left_neg
    curve_neg = 6.0 * (mean_neg - 0.5 * (left_neg + right_neg))
    backward = courant * (left_neg + 0.5 * upwind * (slope_neg + (1.0 - 2.0 * upwind / 3.0) * curve_neg))
    return jnp.where(courant > 0.0, forward, backward)


def zonal_step(field, courant):
    west = jnp.roll(field, 1, -1)
    west_two = jnp.roll(field, 2, -1)
    east = jnp.roll(field, -1, -1)
    faces = (7.0 / 12.0) * (west + field) - (1.0 / 12.0) * (west_two + east)
    flux = ppm_flux(courant, jnp.roll(faces, 1, -1), faces, west, faces, jnp.roll(faces, -1, -1), field)
    return field - (jnp.roll(flux, -1, -1) - flux)


def meridional_step(field, courant):
    count = field.shape[-2]
    faces = (7.0 / 12.0) * (field[..., 1:count - 2, :] + field[..., 2:count - 1, :]) - (1.0 / 12.0) * (field[..., 0:count - 3, :] + field[..., 3:count, :])
    flux = ppm_flux(courant[..., 3:count - 2, :], faces[..., 0:count - 5, :], faces[..., 1:count - 4, :], field[..., 2:count - 3, :], faces[..., 1:count - 4, :], faces[..., 2:count - 3, :], field[..., 3:count - 2, :])
    return field[..., 3:count - 3, :] - (flux[..., 1:, :] - flux[..., :-1, :])


def remap_row(fields, thick, weights):
    bottom = top_pressure + jnp.cumsum(thick, axis=0)
    upper = bottom - thick
    span = bottom[-1] - top_pressure
    share = weights / jnp.sum(weights)
    frac_low = jnp.cumsum(share)
    frac_up = frac_low - share
    target_low = top_pressure + span[None, :] * frac_low[:, None]
    target_up = target_low - span[None, :] * share[:, None]
    intersection = jnp.maximum(0.0, jnp.minimum(bottom[:, None, :], target_low[None]) - jnp.maximum(upper[:, None, :], target_up[None]))
    density = fields / thick[None]
    remapped = jnp.einsum('fjl,jkl->fkl', density, intersection, precision=lax.Precision.HIGHEST)
    theta = remapped[0] / (target_low - target_up)
    layer = gas_factor * theta * jnp.log(target_low / target_up)
    integral = jnp.flip(jnp.cumsum(jnp.flip(layer, 0), 0), 0)
    return remapped, integral


def remap_block(fields, thick, weights):
    def one_row(pair):
        return remap_row(pair[0], pair[1], weights)

    new_rows, integral_rows = lax.map(one_row, (jnp.moveaxis(fields, 2, 0), jnp.moveaxis(thick, 1, 0)))
    return jnp.moveaxis(new_rows, 0, 2), jnp.moveaxis(integral_rows, 0, 1)


def reference(tracers, courant_x, courant_y, thickness, level_weights, surface_geo):
    row_index = jnp.arange(courant_y.shape[1])
    meridional = courant_y * (row_index != 0).astype(courant_y.dtype)[None, :, None]
    widened = jnp.pad(meridional, ((0, 0), (3, 3), (0, 0)))
    field = tracers
    for substep in range(SUBSTEPS):
        field = zonal_step(field, courant_x)
        field = meridional_step(jnp.pad(field, ((0, 0), (0, 0), (3, 3), (0, 0))), widened)
    remapped, integral = remap_block(field, thickness, level_weights)
    return remapped, integral + surface_geo[None]
```

```python
import functools

import jax
import jax.numpy as jnp
from jax import lax
from jax.experimental import pallas as pl
from jax.experimental.pallas import tpu as pltpu
from jax.sharding import PartitionSpec as P

SUBSTEPS = 4
HALO = 3
LANES = 128
TOP_PRESSURE = 1.0
GAS_FACTOR = 0.3


def face_weights(courant):
    size = jnp.abs(courant)
    rest = 1.0 - size
    scaled = courant * rest * (1.0 / 12.0)
    return scaled * rest, scaled * size, courant * size * (3.0 - 2.0 * size)


def stencil_weights(courant):
    p, q, r = face_weights(courant)
    pos = courant > 0.0
    qp, rp = jnp.where(pos, q, 0.0), jnp.where(pos, r, 0.0)
    qn, rn = q - qp, r - rp
    p7 = 7.0 * p
    return [
        qp,
        -p - 7.0 * qp,
        p7 - 7.0 * qp + qn + rp,
        p7 + qp - 7.0 * qn + rn,
        -p - 7.0 * qn,
        qn,
    ]


def kernel(nsuper, rows, nlon, tr, cx, cy, th, wts, sgeo, out, geo,
           send1, recv1, field, zon, wz, wy, cyrow, cytop, thp, thr, col, outp, outr, geop, geor,
           s1, r1, sth, rth, sh, rh, sc, rc, sx, rx, so, ro, sg, rg):
    lat, lev = lax.axis_index("lat"), lax.axis_index("lev")
    sb, l = lat // 2, lat % 2
    h, c = lev // 2, lev % 2
    y = 2 * h + l
    tiles = nlon // LANES
    pieces = [(0, 8), (8, rows - 8)]
    has_low, has_up = sb > 0, sb < nsuper - 1

    def lane(i):
        return pl.ds(pl.multiple_of(i * LANES, LANES), LANES)

    barrier = pltpu.get_barrier_semaphore()
    for k in range(1, 8):
        pl.semaphore_signal(barrier, 1, device_id=(2 * sb + (l ^ (k // 4)), lev ^ (k % 4)))

    @pl.when(has_low)
    def _():
        pl.semaphore_signal(barrier, 1, device_id=(lat - 2, lev))

    @pl.when(has_up)
    def _():
        pl.semaphore_signal(barrier, 1, device_id=(lat + 2, lev))

    def pack(i, _):
        at = lane(i)
        for f in range(8):
            for a in range(2):
                for r0, n in pieces:
                    send1[f // 2, i, pl.ds(r0 * 8 + 2 * (f % 2) + a, n, stride=8), :] = tr[f, a, r0:r0 + n, at]
        for arr, ref in ((2, cx), (3, cy)):
            for a in range(2):
                for r0, n in pieces:
                    piece = ref[a, r0:r0 + n, at]
                    for dest in range(4):
                        send1[dest, i, pl.ds(r0 * 8 + 2 * arr + a, n, stride=8), :] = piece
        for a in range(2):
            thp[i, a * rows:(a + 1) * rows, :] = th[a, :, at]
        return 0

    lax.fori_loop(0, tiles, pack, 0)

    @pl.when(jnp.logical_not(has_low))
    def _():
        for t in range(SUBSTEPS):
            zon[t, :, 0:8 * HALO, :] = jnp.zeros((tiles, 8 * HALO, LANES), jnp.float32)

    @pl.when(jnp.logical_not(has_up))
    def _():
        for t in range(SUBSTEPS):
            zon[t, :, 8 * (HALO + 2 * rows):, :] = jnp.zeros((tiles, 8 * HALO, LANES), jnp.float32)
        cytop[...] = jnp.zeros((tiles, 8, LANES), jnp.float32)

    others = 7 + has_low.astype(jnp.int32) + has_up.astype(jnp.int32)
    pl.semaphore_wait(barrier, others)

    def copy_to(src, dst, ssem, rsem, device):
        return pltpu.make_async_remote_copy(src, dst, ssem, rsem, device_id=device)

    def start(own, src, dst, ssem, rsem, device):
        if own is None:
            copy_to(src, dst, ssem, rsem, device).start()
            return

        @pl.when(own)
        def _():
            pltpu.make_async_copy(src, dst, rsem).start()

        @pl.when(jnp.logical_not(own))
        def _():
            copy_to(src, dst, ssem, rsem, device).start()

    def sent(own, src, dst, ssem, rsem, device):
        if own is None:
            copy_to(src, dst, ssem, rsem, device).wait_send()
            return

        @pl.when(jnp.logical_not(own))
        def _():
            copy_to(src, dst, ssem, rsem, device).wait_send()

    def arrived(dst, rsem):
        pltpu.make_async_copy(dst, dst, rsem).wait()

    moves1, movesth = [], []
    for k in (3, 2, 1, 0):
        hd, ld = h ^ (k // 2), l ^ (k % 2)
        own = None if k else (c == h)
        moves1.append((own, send1.at[2 * hd + ld], recv1.at[2 * l + c], s1.at[k], r1.at[2 * l + c],
                       (2 * sb + ld, 2 * hd + h)))
        own = None if k else (c == l)
        movesth.append((own, thp, thr.at[lev], sth.at[k], rth.at[lev], (2 * sb + ld, 2 * hd + l)))
    for move in moves1:
        start(*move)
    for move in movesth:
        start(*move)

    for slot in range(4):
        arrived(recv1.at[slot], r1.at[slot])

    sub = lax.broadcasted_iota(jnp.int32, (8, LANES), 0)
    col_id = lax.broadcasted_iota(jnp.int32, (8, LANES), 1)
    keep = jnp.where(has_low, 1.0, 0.0)

    def shifted(values, steps):
        count = len(values)
        turned = [pltpu.roll(v, (-steps) % LANES, 1) for v in values]
        if steps < 0:
            return [jnp.where(col_id < -steps, turned[m - 1], turned[m]) for m in range(count)]
        return [jnp.where(col_id >= LANES - steps, turned[(m + 1) % count], turned[m]) for m in range(count)]

    def unpack(r, _):
        at8 = pl.ds(pl.multiple_of(8 * r, 8), 8)
        for band in range(2):
            to8 = pl.ds(pl.multiple_of(8 * (r + band * rows), 8), 8)
            cxs = []
            for m in range(tiles):
                b0, b1 = recv1[2 * band, m, at8, :], recv1[2 * band + 1, m, at8, :]
                half = pltpu.roll(b0, 4, 0)
                field[0, m, to8, :] = jnp.where(sub < 4, b0, pltpu.roll(b1, 4, 0))
                cxs.append(jnp.where(sub < 2, half, jnp.where(sub < 4, pltpu.roll(b0, 6, 0),
                                                              jnp.where(sub < 6, b1, pltpu.roll(b1, 2, 0)))))
                cyr = jnp.where(sub < 2, pltpu.roll(b0, 2, 0),
                                jnp.where(sub < 4, half, jnp.where(sub < 6, pltpu.roll(b1, 6, 0), b1)))
                if band == 0:
                    cyr = jnp.where(r == 0, keep * cyr, cyr)

                    @pl.when(r == 0)
                    def _():
                        cyrow[m] = cyr
                for n, w in enumerate(face_weights(cyr)):
                    wy[n, m, to8, :] = w
            for m, (cxr, cxe) in enumerate(zip(cxs, shifted(cxs, 1))):
                west, east = stencil_weights(cxr), stencil_weights(cxe)
                wz[0, m, to8, :] = west[0]
                for n in range(1, 6):
                    w = west[n] - east[n - 1]
                    wz[n, m, to8, :] = w + 1.0 if n == 3 else w
                wz[6, m, to8, :] = -east[5]
        return 0

    lax.fori_loop(0, rows, unpack, 0)

    def low_row():
        return copy_to(cyrow, cytop, sc, rc, (lat - 2, lev))

    @pl.when(has_low)
    def _():
        low_row().start()

    def zonal(t, r0, n, step):
        def do(i, _):
            for d in range(step):
                row = r0 + i * step + d
                at8 = pl.ds(pl.multiple_of(8 * row, 8), 8)
                f = [field[t, m, at8, :] for m in range(tiles)]
                total = [wz[3, m, at8, :] * f[m] for m in range(tiles)]
                for k in (0, 1, 2, 4, 5, 6):
                    moved = shifted(f, k - 3)
                    total = [total[m] + wz[k, m, at8, :] * moved[m] for m in range(tiles)]
                to8 = pl.ds(pl.multiple_of(8 * (row + HALO), 8), 8)
                for m in range(tiles):
                    zon[t, m, to8, :] = total[m]
            return 0
        lax.fori_loop(0, n // step, do, 0)

    def meridional(t, r0, n):
        def do(i, _):
            def z(row):
                return zon[t, i, 8 * (row + HALO):8 * (row + HALO) + 8, :]

            window = [z(r0 + d) for d in range(-3, 3)]
            sums = [window[m] + window[m + 1] for m in range(5)]
            def face(m):
                return 8.0 * sums[m] - (sums[m - 1] + sums[m + 1])
            values = [face(1), face(2), face(3)]
            before = None
            for row in range(r0, r0 + n + 1):
                at8 = slice(8 * row, 8 * row + 8)
                p, q, r = wy[0, i, at8, :], wy[1, i, at8, :], wy[2, i, at8, :]
                pos = p > 0.0
                flux = p * values[1] - q * jnp.where(pos, values[0], values[2]) + r * jnp.where(
                    pos, window[2], window[3])
                if before is not None:
                    field[t + 1, i, 8 * (row - 1):8 * row, :] = window[2] - (flux - before)
                before = flux
                if row < r0 + n:
                    window = window[1:] + [z(row + 3)]
                    sums = sums[1:] + [window[4] + window[5]]
                    values = values[1:] + [face(3)]
            return 0
        lax.fori_loop(0, tiles, do, 0)

    edge = 8 * HALO
    top = 8 * 2 * rows

    def to_low(t):
        return copy_to(zon.at[t, :, pl.ds(edge, edge)], zon.at[t, :, pl.ds(edge + top, edge)],
                       sh.at[t, 0], rh.at[t, 0], (lat - 2, lev))

    def to_up(t):
        return copy_to(zon.at[t, :, pl.ds(top, edge)], zon.at[t, :, pl.ds(0, edge)],
                       sh.at[t, 1], rh.at[t, 1], (lat + 2, lev))

    def edges(t):
        zonal(t, 0, HALO, HALO)

        @pl.when(has_low)
        def _():
            to_low(t).start()
        zonal(t, 2 * rows - HALO, HALO, HALO)

        @pl.when(has_up)
        def _():
            to_up(t).start()

    edges(0)
    for t in range(SUBSTEPS):
        zonal(t, HALO, 2 * rows - 2 * HALO, 3)
        if t == 0:
            @pl.when(has_up)
            def _():
                low_row().wait_recv()
            for n, w in enumerate(face_weights(cytop[...])):
                wy[n, :, top:top + 8, :] = w
        meridional(t, HALO, 2 * rows - 2 * HALO)

        @pl.when(has_low)
        def _():
            to_up(t).wait_recv()
        meridional(t, 0, HALO)

        @pl.when(has_up)
        def _():
            to_low(t).wait_recv()
        meridional(t, 2 * rows - HALO, HALO)
        if t + 1 < SUBSTEPS:
            edges(t + 1)

    part = 8 * rows
    swap = copy_to(field.at[SUBSTEPS, :, pl.ds(pl.multiple_of((1 - c) * part, part), part)], col.at[c],
                   sx, rx, (lat, lev ^ 1))
    swap.start()
    col[c] = field[SUBSTEPS, :, pl.ds(pl.multiple_of(c * part, part), part), :]
    for slot in range(4):
        arrived(thr.at[slot], rth.at[slot])
    swap.wait_recv()

    def remap(i, _):
        for r0, n in pieces:
            shape = (n, LANES)
            weights = [jnp.full(shape, wts[k], jnp.float32) for k in range(8)]
            whole = weights[0]
            for k in range(1, 8):
                whole = whole + weights[k]
            inverse = 1.0 / whole
            thick = [thr[j // 2, i, (j % 2) * rows + r0:(j % 2) * rows + r0 + n, :] for j in range(8)]
            bounds = [jnp.full(shape, TOP_PRESSURE, jnp.float32)]
            for j in range(8):
                bounds.append(bounds[-1] + thick[j])
            span = bounds[8] - TOP_PRESSURE
            low, up, total = [], [], None
            for k in range(8):
                total = weights[k] if total is None else total + weights[k]
                low.append(TOP_PRESSURE + span * (total * inverse))
                up.append(low[k] - span * (weights[k] * inverse))
            density = [[], []]
            for j in range(8):
                reciprocal = 1.0 / thick[j]
                for f in range(2):
                    sublane = 4 * ((j % 4) // 2) + 2 * f + j % 2
                    density[f].append(col[j // 4, i, pl.ds(r0 * 8 + sublane, n, stride=8), :] * reciprocal)
            for k in range(8):
                sums = [None, None]
                for j in range(8):
                    cut = jnp.maximum(0.0, jnp.minimum(bounds[j + 1], low[k]) - jnp.maximum(bounds[j], up[k]))
                    for f in range(2):
                        term = density[f][j] * cut
                        sums[f] = term if sums[f] is None else sums[f] + term
                for f in range(2):
                    outp[k // 2, i, pl.ds(r0 * 4 + 2 * f + k % 2, n, stride=4), :] = sums[f]
                density_k = sums[0]
                low_k = low[k]
                up_k = up[k]

                @pl.when(y == 0)
                def _():
                    geop[k // 2, i, (k % 2) * rows + r0:(k % 2) * rows + r0 + n, :] = (
                        GAS_FACTOR * density_k / (low_k - up_k) * jnp.log(low_k / up_k))
        return 0

    lax.fori_loop(0, tiles, remap, 0)

    moves2, movesg = [], []
    for k in (3, 2, 1, 0):
        gd = lev ^ k
        moves2.append((None if k else (c == l), outp.at[gd], outr.at[y], so.at[k], ro.at[y], (2 * sb + c, gd)))
        movesg.append((None if k else (c == l), geop.at[gd], geor, sg.at[k], rg, (2 * sb + c, gd)))
    for move in moves2:
        start(*move)

    @pl.when(y == 0)
    def _():
        def integrate(i, _):
            total = None
            for k in range(7, -1, -1):
                here = slice((k % 2) * rows, (k % 2) * rows + rows)
                layer = geop[k // 2, i, here, :]
                total = layer if total is None else total + layer
                geop[k // 2, i, here, :] = total
            return 0
        lax.fori_loop(0, tiles, integrate, 0)
        for move in movesg:
            start(*move)

    for slot in range(4):
        arrived(outr.at[slot], ro.at[slot])

    def finish(i, _):
        at = lane(i)
        for f in range(8):
            for a in range(2):
                for r0, n in pieces:
                    out[f, a, r0:r0 + n, at] = outr[f // 2, i, pl.ds(r0 * 4 + 2 * (f % 2) + a, n, stride=4), :]
        return 0

    lax.fori_loop(0, tiles, finish, 0)
    arrived(geor, rg)

    def finish_geo(i, _):
        at = lane(i)
        for a in range(2):
            geo[a, :, at] = geor[i, a * rows:(a + 1) * rows, :] + sgeo[:, at]
        return 0

    lax.fori_loop(0, tiles, finish_geo, 0)

    for move in moves1 + movesth + moves2:
        sent(*move)

    @pl.when(y == 0)
    def _():
        for move in movesg:
            sent(*move)
    swap.wait_send()

    @pl.when(has_low)
    def _():
        low_row().wait_send()
        for t in range(SUBSTEPS):
            to_low(t).wait_send()

    @pl.when(has_up)
    def _():
        for t in range(SUBSTEPS):
            to_up(t).wait_send()


def body(nsuper, tracers, courant_x, courant_y, thickness, level_weights, surface_geo):
    rows, nlon = tracers.shape[2:]
    f32 = jnp.float32
    vmem = pl.BlockSpec(memory_space=pltpu.VMEM)

    def buffer(count, height):
        return pltpu.VMEM((count, nlon // LANES, height, LANES), f32)

    def single(height):
        return pltpu.VMEM((nlon // LANES, height, LANES), f32)

    dma = pltpu.SemaphoreType.DMA
    both = 2 * rows
    scratch = [
        buffer(4, 8 * rows), buffer(4, 8 * rows), buffer(SUBSTEPS + 1, 8 * both),
        buffer(SUBSTEPS, 8 * (both + 2 * HALO)), buffer(7, 8 * both), buffer(3, 8 * (both + 1)),
        single(8), single(8), single(both), buffer(4, both), buffer(2, 8 * rows),
        buffer(4, 4 * rows), buffer(4, 4 * rows), buffer(4, both), single(both),
        dma((4,)), dma((4,)), dma((4,)), dma((4,)), dma((SUBSTEPS, 2)), dma((SUBSTEPS, 2)), dma, dma, dma, dma,
        dma((4,)), dma((4,)), dma((4,)), dma,
    ]
    return pl.pallas_call(
        functools.partial(kernel, nsuper, rows, nlon),
        out_shape=(jax.ShapeDtypeStruct(tracers.shape, f32), jax.ShapeDtypeStruct(thickness.shape, f32)),
        in_specs=[vmem] * 4 + [pl.BlockSpec(memory_space=pltpu.SMEM), vmem],
        out_specs=(vmem, vmem),
        scratch_shapes=scratch,
        compiler_params=pltpu.CompilerParams(
            collective_id=0, has_side_effects=True, vmem_limit_bytes=50 * 2**20),
        name="transport_remap",
    )(tracers, courant_x, courant_y, thickness, level_weights, surface_geo)


def solution(mesh):
    in_specs = (
        P(None, "lev", "lat", None),
        P("lev", "lat", None),
        P("lev", "lat", None),
        P("lev", "lat", None),
        P(),
        P("lat", None),
    )
    out_specs = (P(None, "lev", "lat", None), P("lev", "lat", None))
    run = functools.partial(body, mesh.shape["lat"] // 2)
    return jax.shard_map(run, mesh=mesh, in_specs=in_specs, out_specs=out_specs, check_vma=False)
```

```python
import functools

import jax
import jax.numpy as jnp
from jax import lax
from jax.experimental import pallas as pl
from jax.experimental.layout import Layout, with_layout_constraint
from jax.experimental.pallas import tpu as pltpu
from jax.sharding import PartitionSpec as P

SUBSTEPS = 4
HALO = 3
CHUNK = 4
LANES = 128
TOP_PRESSURE = 1.0
GAS_FACTOR = 0.3


def face_weights(courant):
    size = jnp.abs(courant)
    rest = 1.0 - size
    scaled = courant * rest * (1.0 / 12.0)
    return scaled * rest, scaled * size, courant * size * (3.0 - 2.0 * size)


def stencil_weights(courant):
    p, q, r = face_weights(courant)
    pos = courant > 0.0
    qp, rp = jnp.where(pos, q, 0.0), jnp.where(pos, r, 0.0)
    qn, rn = q - qp, r - rp
    p7 = 7.0 * p
    return [
        qp,
        -p - 7.0 * qp,
        p7 - 7.0 * qp + qn + rp,
        p7 + qp - 7.0 * qn + rn,
        -p - 7.0 * qn,
        qn,
    ]


def kernel(nsuper, rows, tiles, tr, cx, cy, th, wts_hbm, out, geor, wts, lsem,
           recvf, recvx, recvy, thr, field, zon, cxt, cyt, wz, wy, cyrow, cytop, tht, col, tmp, outp, geop,
           s1, r1, sth, rth, sh, rh, sc, rc, sx, rx, so, ro, sg, rg):
    lat, lev = lax.axis_index("lat"), lax.axis_index("lev")
    sb, l = lat // 2, lat % 2
    h, c = lev // 2, lev % 2
    y = 2 * h + l
    both = 2 * rows
    chunks = rows // CHUNK
    pitch = 2 * tiles
    lines = CHUNK * pitch
    has_low, has_up = sb > 0, sb < nsuper - 1

    weights_copy = pltpu.make_async_copy(wts_hbm, wts, lsem)
    weights_copy.start()

    barrier = pltpu.get_barrier_semaphore()
    for k in range(1, 8):
        pl.semaphore_signal(barrier, 1, device_id=(2 * sb + (l ^ (k // 4)), lev ^ (k % 4)))

    @pl.when(has_low)
    def _():
        pl.semaphore_signal(barrier, 1, device_id=(lat - 2, lev))

    @pl.when(has_up)
    def _():
        pl.semaphore_signal(barrier, 1, device_id=(lat + 2, lev))

    @pl.when(jnp.logical_not(has_low))
    def _():
        for t in range(SUBSTEPS):
            zon[t, :, 0:8 * HALO, :] = jnp.zeros((tiles, 8 * HALO, LANES), jnp.float32)

    @pl.when(jnp.logical_not(has_up))
    def _():
        for t in range(SUBSTEPS):
            zon[t, :, 8 * (HALO + both):, :] = jnp.zeros((tiles, 8 * HALO, LANES), jnp.float32)
        cytop[...] = jnp.zeros((tiles, 8, LANES), jnp.float32)

    others = 7 + has_low.astype(jnp.int32) + has_up.astype(jnp.int32)
    pl.semaphore_wait(barrier, others)

    def copy_to(src, dst, ssem, rsem, device):
        return pltpu.make_async_remote_copy(src, dst, ssem, rsem, device_id=device)

    def start(own, src, dst, ssem, rsem, device):
        if own is None:
            copy_to(src, dst, ssem, rsem, device).start()
            return

        @pl.when(own)
        def _():
            pltpu.make_async_copy(src, dst, rsem).start()

        @pl.when(jnp.logical_not(own))
        def _():
            copy_to(src, dst, ssem, rsem, device).start()

    def sent(own, src, dst, ssem, rsem, device):
        if own is None:
            copy_to(src, dst, ssem, rsem, device).wait_send()
            return

        @pl.when(jnp.logical_not(own))
        def _():
            copy_to(src, dst, ssem, rsem, device).wait_send()

    def arrived(dst, rsem):
        pltpu.make_async_copy(dst, dst, rsem).wait()

    def place(band, j):
        if isinstance(band, int):
            return j * CHUNK if band == 0 else rows - (j + 1) * CHUNK
        return jnp.where(band == 0, j * CHUNK, rows - (j + 1) * CHUNK)

    def span_of(band, j):
        first = place(band, j) * pitch
        return pl.ds(first if isinstance(first, int) else pl.multiple_of(first, 8), lines)

    moves = []
    slot = 2 * l + c
    for j in range(chunks):
        here = span_of(l, j)
        groups = [[], [], []]
        for k in (3, 2, 1, 0):
            hd, ld = h ^ (k // 2), l ^ (k % 2)
            own = None if k else (c == h)
            device = (2 * sb + ld, 2 * hd + h)
            groups[0].append((own, tr.at[pl.ds(2 * (2 * hd + ld), 2), here], recvf.at[slot, :, here],
                              s1.at[0, j, k], r1.at[0, j, slot], device))
            groups[1].append((own, cx.at[here], recvx.at[slot, here], s1.at[1, j, k], r1.at[1, j, slot], device))
            groups[2].append((own, cy.at[here], recvy.at[slot, here], s1.at[2, j, k], r1.at[2, j, slot], device))
        for group in groups:
            moves += group
    for k in (3, 2, 1, 0):
        hd, ld = h ^ (k // 2), l ^ (k % 2)
        own = None if k else (c == l)
        moves.append((own, th, thr.at[lev], sth.at[k], rth.at[lev], (2 * sb + ld, 2 * hd + l)))
    for move in moves:
        start(*move)

    weights_copy.wait()

    col_id = lax.broadcasted_iota(jnp.int32, (8, LANES), 1)
    keep = jnp.where(has_low, 1.0, 0.0)

    def shifted(values, steps):
        count = len(values)
        turned = [pltpu.roll(v, (-steps) % LANES, 1) for v in values]
        if steps < 0:
            return [jnp.where(col_id < -steps, turned[m - 1], turned[m]) for m in range(count)]
        return [jnp.where(col_id >= LANES - steps, turned[(m + 1) % count], turned[m]) for m in range(count)]

    def unpack(j, source, target, twice):
        def do(i, _):
            for band in range(2):
                r0 = place(band, j)
                for pair in range(2):
                    for a in range(2):
                        for f in range(2):
                            line = pl.ds(r0 * pitch + 2 * i + a, CHUNK, stride=pitch)
                            ref = source.at[2 * band + pair] if twice else source.at[2 * band + pair, f]
                            target[i, pl.ds(8 * (band * rows + r0) + 4 * f + 2 * pair + a, CHUNK, stride=8), :] = ref[line, :]
            return 0
        lax.fori_loop(0, tiles, do, 0)

    def both_places(j):
        return [place(0, j), rows + place(1, j)]

    def at_row(row):
        return pl.ds(8 * row if isinstance(row, int) else pl.multiple_of(8 * row, 8), 8)

    def zonal_weights(j):
        def do(d, _):
            for first in both_places(j):
                at8 = at_row(first + d)
                cxs = [cxt[m, at8, :] for m in range(tiles)]
                for m, (cxr, cxe) in enumerate(zip(cxs, shifted(cxs, 1))):
                    west, east = stencil_weights(cxr), stencil_weights(cxe)
                    wz[0, m, at8, :] = west[0]
                    for n in range(1, 6):
                        w = west[n] - east[n - 1]
                        wz[n, m, at8, :] = w + 1.0 if n == 3 else w
                    wz[6, m, at8, :] = -east[5]
            return 0
        lax.fori_loop(0, CHUNK, do, 0)

    def meridional_weights(j):
        def do(i, _):
            for first in both_places(j):
                for d in range(CHUNK):
                    at8 = at_row(first + d)
                    cyr = cyt[i, at8, :]
                    if first + d == 0:
                        cyr = keep * cyr
                        cyrow[i] = cyr
                    for n, w in enumerate(face_weights(cyr)):
                        wy[n, i, at8, :] = w
            return 0
        lax.fori_loop(0, tiles, do, 0)

    def low_row():
        return copy_to(cyrow, cytop, sc, rc, (lat - 2, lev))

    def zonal(t, starts, n, step):
        def do(i, _):
            for first in starts:
                for d in range(step):
                    row = first + i * step + d
                    at8 = at_row(row)
                    f = [field[t, m, at8, :] for m in range(tiles)]
                    total = [wz[3, m, at8, :] * f[m] for m in range(tiles)]
                    for k in (0, 1, 2, 4, 5, 6):
                        moved = shifted(f, k - 3)
                        total = [total[m] + wz[k, m, at8, :] * moved[m] for m in range(tiles)]
                    to8 = at_row(row + HALO)
                    for m in range(tiles):
                        zon[t, m, to8, :] = total[m]
            return 0
        if n == step:
            do(0, 0)
        else:
            lax.fori_loop(0, n // step, do, 0)

    def meridional(t, starts, n):
        def do(i, _):
            for r0 in starts:
                def z(row):
                    return zon[t, i, 8 * (row + HALO):8 * (row + HALO) + 8, :]

                window = [z(r0 + d) for d in range(-3, 3)]
                sums = [window[m] + window[m + 1] for m in range(5)]

                def face(m):
                    return 8.0 * sums[m] - (sums[m - 1] + sums[m + 1])
                values = [face(1), face(2), face(3)]
                before = None
                for row in range(r0, r0 + n + 1):
                    at8 = at_row(row)
                    p, q, r = wy[0, i, at8, :], wy[1, i, at8, :], wy[2, i, at8, :]
                    pos = p > 0.0
                    flux = p * values[1] - q * jnp.where(pos, values[0], values[2]) + r * jnp.where(
                        pos, window[2], window[3])
                    if before is not None:
                        field[t + 1, i, at_row(row - 1), :] = window[2] - (flux - before)
                    before = flux
                    if row < r0 + n:
                        window = window[1:] + [z(row + 3)]
                        sums = sums[1:] + [window[4] + window[5]]
                        values = values[1:] + [face(3)]
            return 0
        lax.fori_loop(0, tiles, do, 0)

    edge = 8 * HALO
    top = 8 * both
    ends = [0, both - HALO]

    def to_low(t):
        return copy_to(zon.at[t, :, pl.ds(edge, edge)], zon.at[t, :, pl.ds(edge + top, edge)],
                       sh.at[t, 0], rh.at[t, 0], (lat - 2, lev))

    def to_up(t):
        return copy_to(zon.at[t, :, pl.ds(top, edge)], zon.at[t, :, pl.ds(0, edge)],
                       sh.at[t, 1], rh.at[t, 1], (lat + 2, lev))

    def send_halo(t):
        zonal(t, ends, HALO, HALO)

        @pl.when(has_low)
        def _():
            to_low(t).start()

        @pl.when(has_up)
        def _():
            to_up(t).start()

    def wait_halo(t):
        @pl.when(has_low)
        def _():
            to_up(t).wait_recv()

        @pl.when(has_up)
        def _():
            to_low(t).wait_recv()

    def take_fields(j):
        for kind, ref in ((0, recvf), (1, recvx)):
            for s in range(4):
                for band in range(2):
                    if s // 2 == band:
                        here = span_of(band, j)
                        arrived(ref.at[s, :, here] if kind == 0 else ref.at[s, here], r1.at[kind, j, s])
        unpack(j, recvx, cxt, True)
        unpack(j, recvf, field.at[0], False)
        zonal_weights(j)

    def take_courant(j):
        for s in range(4):
            arrived(recvy.at[s, span_of(s // 2, j)], r1.at[2, j, s])
        unpack(j, recvy, cyt, True)
        meridional_weights(j)

    part = 8 * CHUNK

    def swap(j):
        theirs = pl.multiple_of(8 * ((1 - c) * rows + place(1 - c, j)), part)
        return copy_to(field.at[SUBSTEPS, :, pl.ds(theirs, part)], col.at[c, j], sx.at[j], rx.at[j], (lat, lev ^ 1))

    def send_swap(j):
        swap(j).start()
        ours = pl.multiple_of(8 * (c * rows + place(c, j)), part)
        col[c, j] = field[SUBSTEPS, :, pl.ds(ours, part), :]

    full = (8, LANES)

    def take_thickness():
        for s in range(4):
            arrived(thr.at[s], rth.at[s])

        def do(i, _):
            for j in range(chunks):
                first = place(c, j) * pitch + 2 * i
                for k in range(8):
                    piece = thr[k // 2, pl.ds(first + k % 2, CHUNK, stride=pitch), :]
                    for f in range(2):
                        tht[j, i, pl.ds(8 * k + f, CHUNK, stride=2), :] = piece
            return 0
        lax.fori_loop(0, tiles, do, 0)

    def columns(j, i):
        weights = [jnp.full(full, wts[k], jnp.float32) for k in range(8)]
        whole = weights[0]
        for k in range(1, 8):
            whole = whole + weights[k]
        inverse = 1.0 / whole
        thick = [tht[j, i, 8 * k:8 * k + 8, :] for k in range(8)]
        bounds = [jnp.full(full, TOP_PRESSURE, jnp.float32)]
        for k in range(8):
            bounds.append(bounds[-1] + thick[k])
        span = bounds[8] - TOP_PRESSURE
        low, up, total = [], [], None
        for k in range(8):
            total = weights[k] if total is None else total + weights[k]
            low.append(TOP_PRESSURE + span * (total * inverse))
            up.append(low[k] - span * (weights[k] * inverse))
        return thick, bounds, low, up

    def remap(j):
        def do(i, _):
            thick, bounds, low, up = columns(j, i)
            density = [col[k // 4, j, i, pl.ds(k % 4, 8, stride=4), :] / thick[k] for k in range(8)]
            for k in range(8):
                total = None
                for n in range(8):
                    cut = jnp.maximum(0.0, jnp.minimum(bounds[n + 1], low[k]) - jnp.maximum(bounds[n], up[k]))
                    total = density[n] * cut if total is None else total + density[n] * cut
                tmp[i, 8 * k:8 * k + 8, :] = total
            for k in range(8):
                for f in range(2):
                    outp[k // 2, j, f, pl.ds(2 * i + k % 2, CHUNK, stride=pitch), :] = (
                        tmp[i, pl.ds(8 * k + f, CHUNK, stride=2), :])
            return 0
        lax.fori_loop(0, tiles, do, 0)

    def integrate(j):
        def do(i, _):
            _, _, low, up = columns(j, i)
            total = None
            for k in range(7, -1, -1):
                layer = GAS_FACTOR * tmp[i, 8 * k:8 * k + 8, :] / (low[k] - up[k]) * jnp.log(low[k] / up[k])
                total = layer if total is None else total + layer
                tmp[i, 8 * k:8 * k + 8, :] = total
            for k in range(8):
                geop[k // 2, j, pl.ds(2 * i + k % 2, CHUNK, stride=pitch), :] = (
                    tmp[i, pl.ds(8 * k, CHUNK, stride=2), :])
            return 0
        lax.fori_loop(0, tiles, do, 0)

    def result_moves(j):
        here = span_of(c, j)
        for k in (3, 2, 1, 0):
            gd = lev ^ k
            yield (None if k else (c == l), outp.at[gd, j], out.at[pl.ds(2 * y, 2), here],
                   so.at[j, k], ro.at[j, y], (2 * sb + c, gd))

    def integral_moves(j):
        here = span_of(c, j)
        for k in (3, 2, 1, 0):
            gd = lev ^ k
            yield (None if k else (c == l), geop.at[gd, j], geor.at[here], sg.at[j, k], rg.at[j], (2 * sb + c, gd))

    def send_results(j):
        swap(j).wait_recv()
        remap(j)
        for move in result_moves(j):
            start(*move)

        @pl.when(y == 0)
        def _():
            integrate(j)
            for move in integral_moves(j):
                start(*move)

    take_fields(0)
    send_halo(0)
    zonal(0, [HALO, both - HALO - 1], 1, 1)
    take_courant(0)

    @pl.when(has_low)
    def _():
        low_row().start()

    take_fields(1)
    zonal(0, both_places(1), CHUNK, CHUNK)
    take_courant(1)

    @pl.when(has_up)
    def _():
        low_row().wait_recv()
    for n, w in enumerate(face_weights(cytop[...])):
        wy[n, :, top:top + 8, :] = w
    wait_halo(0)
    meridional(0, [0, both - 5], 5)
    send_halo(1)
    zonal(1, [HALO, both - 5], 2, 2)

    take_fields(2)
    zonal(0, both_places(2), CHUNK, CHUNK)
    take_courant(2)
    meridional(0, [5], both - 10)
    zonal(1, [5, 12], 7, 1)
    wait_halo(1)
    meridional(1, ends, HALO)
    send_halo(2)
    meridional(1, [HALO], both - 2 * HALO)
    zonal(2, [HALO], both - 2 * HALO, 6)
    meridional(2, [5], both - 10)
    zonal(3, [5, 12], 7, 1)
    meridional(3, [8], 8)
    send_swap(2)

    wait_halo(2)
    meridional(2, ends, HALO)
    send_halo(3)
    take_thickness()
    send_results(2)
    meridional(2, [HALO, both - 5], 2)
    zonal(3, [HALO, both - 5], 2, 2)
    meridional(3, [HALO, both - 8], 5)
    send_swap(1)
    send_results(1)

    wait_halo(3)
    meridional(3, ends, HALO)
    send_swap(0)
    send_results(0)

    for j in range(chunks):
        arrived(geor.at[span_of(l, j)], rg.at[j])
    for j in range(chunks):
        for s in range(4):
            arrived(out.at[pl.ds(2 * s, 2), span_of(l, j)], ro.at[j, s])

    for move in moves:
        sent(*move)
    for j in range(chunks):
        swap(j).wait_send()
        for move in result_moves(j):
            sent(*move)

    @pl.when(y == 0)
    def _():
        for j in range(chunks):
            for move in integral_moves(j):
                sent(*move)

    @pl.when(has_low)
    def _():
        low_row().wait_send()
        for t in range(SUBSTEPS):
            to_low(t).wait_send()

    @pl.when(has_up)
    def _():
        for t in range(SUBSTEPS):
            to_up(t).wait_send()


def finish(rows, tiles, result, integral, surface, out, geo, held, total, sgeo, sems, gsems):
    loads = [pltpu.make_async_copy(integral, total, gsems.at[0]), pltpu.make_async_copy(surface, sgeo, gsems.at[1])]
    takes = [pltpu.make_async_copy(result.at[f], held.at[f], sems.at[0, f]) for f in range(8)]
    gives = [pltpu.make_async_copy(held.at[f], out.at[f], sems.at[1, f]) for f in range(8)]
    for copy in loads + takes:
        copy.start()
    for copy in loads:
        copy.wait()
    pitch = 2 * tiles
    for i in range(tiles):
        for r0, n in ((0, 8), (8, rows - 8)):
            piece = sgeo[r0:r0 + n, i * LANES:(i + 1) * LANES]
            for a in range(2):
                here = pl.ds(r0 * pitch + 2 * i + a, n, stride=pitch)
                total[here, :] = total[here, :] + piece
    store = pltpu.make_async_copy(total, geo, gsems.at[2])
    store.start()
    for take, give in zip(takes, gives):
        take.wait()
        give.start()
    for copy in gives + [store]:
        copy.wait()


def in_lines(array):
    lead = array.ndim - 3
    levels, rows, nlon = array.shape[lead:]
    tiles = nlon // LANES
    split = array.reshape(array.shape[:-1] + (tiles, LANES))
    order = tuple(range(lead)) + (lead + 1, lead + 2, lead, lead + 3)
    split = with_layout_constraint(split, Layout(major_to_minor=order))
    return jnp.transpose(split, order).reshape(array.shape[:lead] + (rows * tiles * levels, LANES))


def from_lines(array, levels, rows):
    lead = array.ndim - 2
    tiles = array.shape[-2] // (levels * rows)
    split = array.reshape(array.shape[:lead] + (rows, tiles, levels, LANES))
    split = jnp.transpose(split, tuple(range(lead)) + (lead + 2, lead, lead + 1, lead + 3))
    order = tuple(range(lead)) + (lead + 1, lead + 2, lead, lead + 3)
    split = with_layout_constraint(split, Layout(major_to_minor=order))
    return split.reshape(array.shape[:lead] + (levels, rows, tiles * LANES))


def body(nsuper, tracers, courant_x, courant_y, thickness, level_weights, surface_geo):
    levels, rows, nlon = thickness.shape
    tiles = nlon // LANES
    f32 = jnp.float32
    hbm = pl.BlockSpec(memory_space=pltpu.HBM)
    both = 2 * rows
    lines = rows * tiles * levels
    chunks = rows // CHUNK

    def buffer(*shape):
        return pltpu.VMEM(shape + (LANES,), f32)

    dma = pltpu.SemaphoreType.DMA
    scratch = [
        pltpu.SMEM((8,), f32), dma,
        buffer(4, 2, lines), buffer(4, lines), buffer(4, lines), buffer(4, lines),
        buffer(SUBSTEPS + 1, tiles, 8 * both), buffer(SUBSTEPS, tiles, 8 * (both + 2 * HALO)),
        buffer(tiles, 8 * both), buffer(tiles, 8 * both),
        buffer(7, tiles, 8 * both), buffer(3, tiles, 8 * (both + 1)),
        buffer(tiles, 8), buffer(tiles, 8), buffer(chunks, tiles, 64),
        buffer(2, chunks, tiles, 8 * CHUNK), buffer(tiles, 64),
        buffer(4, chunks, 2, lines // chunks), buffer(4, chunks, lines // chunks),
        dma((3, chunks, 4)), dma((3, chunks, 4)), dma((4,)), dma((4,)), dma((SUBSTEPS, 2)), dma((SUBSTEPS, 2)),
        dma, dma, dma((chunks,)), dma((chunks,)),
        dma((chunks, 4)), dma((chunks, 4)), dma((chunks, 4)), dma((chunks,)),
    ]
    result, integral = pl.pallas_call(
        functools.partial(kernel, nsuper, rows, tiles),
        out_shape=(jax.ShapeDtypeStruct((8, lines, LANES), f32), jax.ShapeDtypeStruct((lines, LANES), f32)),
        in_specs=[hbm] * 5,
        out_specs=(hbm, hbm),
        scratch_shapes=scratch,
        compiler_params=pltpu.CompilerParams(
            collective_id=0, has_side_effects=True, vmem_limit_bytes=60 * 2**20),
        name="transport_remap",
    )(in_lines(tracers), in_lines(courant_x), in_lines(courant_y), in_lines(thickness), level_weights)
    out, geo = pl.pallas_call(
        functools.partial(finish, rows, tiles),
        out_shape=(jax.ShapeDtypeStruct((8, lines, LANES), f32), jax.ShapeDtypeStruct((lines, LANES), f32)),
        in_specs=[hbm] * 3,
        out_specs=(hbm, hbm),
        scratch_shapes=[buffer(8, lines), buffer(lines), pltpu.VMEM((rows, nlon), f32), dma((2, 8)), dma((3,))],
        compiler_params=pltpu.CompilerParams(vmem_limit_bytes=60 * 2**20),
        name="finish",
    )(result, integral, surface_geo)
    return from_lines(out, levels, rows), from_lines(geo, levels, rows)


def solution(mesh):
    in_specs = (
        P(None, "lev", "lat", None),
        P("lev", "lat", None),
        P("lev", "lat", None),
        P("lev", "lat", None),
        P(),
        P("lat", None),
    )
    out_specs = (P(None, "lev", "lat", None), P("lev", "lat", None))
    run = functools.partial(body, mesh.shape["lat"] // 2)
    return jax.shard_map(run, mesh=mesh, in_specs=in_specs, out_specs=out_specs, check_vma=False)
```

```python
import functools

import jax
import jax.numpy as jnp
from jax import lax
from jax.experimental import pallas as pl
from jax.experimental.layout import Layout, with_layout_constraint
from jax.experimental.pallas import tpu as pltpu
from jax.sharding import PartitionSpec as P

SUBSTEPS = 4
HALO = 3
CHUNK = 4
LANES = 128
TOP_PRESSURE = 1.0
GAS_FACTOR = 0.3
SHIFTS = (-3, -2, 2, 3)


def face_weights(courant):
    size = jnp.abs(courant)
    rest = 1.0 - size
    scaled = courant * rest * (1.0 / 12.0)
    return scaled * rest, scaled * size, courant * size * (3.0 - 2.0 * size)


def stencil_weights(courant):
    p, q, r = face_weights(courant)
    pos = courant > 0.0
    qp, rp = jnp.where(pos, q, 0.0), jnp.where(pos, r, 0.0)
    qn, rn = q - qp, r - rp
    p7 = 7.0 * p
    return [
        qp,
        -p - 7.0 * qp,
        p7 - 7.0 * qp + qn + rp,
        p7 + qp - 7.0 * qn + rn,
        -p - 7.0 * qn,
        qn,
    ]


def kernel(nsuper, rows, tiles, tr, cx, cy, th, wts_hbm, out, geor, wts, lsem,
           recvf, recvx, recvy, thr, field, zon, cxt, cyt, wz, wy, cyrow, cytop, tht, col, tmp, outp, geop, turns,
           s1, r1, sth, rth, sh, rh, sc, rc, sx, rx, so, ro, sg, rg):
    lat, lev = lax.axis_index("lat"), lax.axis_index("lev")
    sb, l = lat // 2, lat % 2
    h, c = lev // 2, lev % 2
    y = 2 * h + l
    both = 2 * rows
    chunks = rows // CHUNK
    pitch = 2 * tiles
    lines = CHUNK * pitch
    has_low, has_up = sb > 0, sb < nsuper - 1

    weights_copy = pltpu.make_async_copy(wts_hbm, wts, lsem)
    weights_copy.start()

    barrier = pltpu.get_barrier_semaphore()
    for k in range(1, 8):
        pl.semaphore_signal(barrier, 1, device_id=(2 * sb + (l ^ (k // 4)), lev ^ (k % 4)))

    @pl.when(has_low)
    def _():
        pl.semaphore_signal(barrier, 1, device_id=(lat - 2, lev))

    @pl.when(has_up)
    def _():
        pl.semaphore_signal(barrier, 1, device_id=(lat + 2, lev))

    @pl.when(jnp.logical_not(has_low))
    def _():
        for t in range(SUBSTEPS):
            zon[t, :, 0:8 * HALO, :] = jnp.zeros((tiles, 8 * HALO, LANES), jnp.float32)

    @pl.when(jnp.logical_not(has_up))
    def _():
        for t in range(SUBSTEPS):
            zon[t, :, 8 * (HALO + both):, :] = jnp.zeros((tiles, 8 * HALO, LANES), jnp.float32)
        cytop[...] = jnp.zeros((tiles, 8, LANES), jnp.float32)

    source = lax.broadcasted_iota(jnp.int32, (2 * LANES, LANES), 0) % LANES
    target = lax.broadcasted_iota(jnp.int32, (2 * LANES, LANES), 1)
    for n, steps in enumerate(SHIFTS):
        turns[:, n * LANES:(n + 1) * LANES] = jnp.where(
            source == (target + (steps + LANES)) % LANES, 1.0, 0.0).astype(jnp.bfloat16)

    others = 7 + has_low.astype(jnp.int32) + has_up.astype(jnp.int32)
    pl.semaphore_wait(barrier, others)

    def copy_to(src, dst, ssem, rsem, device):
        return pltpu.make_async_remote_copy(src, dst, ssem, rsem, device_id=device)

    def start(own, src, dst, ssem, rsem, device):
        if own is None:
            copy_to(src, dst, ssem, rsem, device).start()
            return

        @pl.when(own)
        def _():
            pltpu.make_async_copy(src, dst, rsem).start()

        @pl.when(jnp.logical_not(own))
        def _():
            copy_to(src, dst, ssem, rsem, device).start()

    def sent(own, src, dst, ssem, rsem, device):
        if own is None:
            copy_to(src, dst, ssem, rsem, device).wait_send()
            return

        @pl.when(jnp.logical_not(own))
        def _():
            copy_to(src, dst, ssem, rsem, device).wait_send()

    def arrived(dst, rsem):
        pltpu.make_async_copy(dst, dst, rsem).wait()

    def place(band, j):
        if isinstance(band, int):
            return j * CHUNK if band == 0 else rows - (j + 1) * CHUNK
        return jnp.where(band == 0, j * CHUNK, rows - (j + 1) * CHUNK)

    def span_of(band, j):
        first = place(band, j) * pitch
        return pl.ds(first if isinstance(first, int) else pl.multiple_of(first, 8), lines)

    moves = []
    slot = 2 * l + c
    for j in range(chunks):
        here = span_of(l, j)
        groups = [[], [], []]
        for k in (3, 2, 1, 0):
            hd, ld = h ^ (k // 2), l ^ (k % 2)
            own = None if k else (c == h)
            device = (2 * sb + ld, 2 * hd + h)
            groups[0].append((own, tr.at[pl.ds(2 * (2 * hd + ld), 2), here], recvf.at[slot, :, here],
                              s1.at[0, j, k], r1.at[0, j, slot], device))
            groups[1].append((own, cx.at[here], recvx.at[slot, here], s1.at[1, j, k], r1.at[1, j, slot], device))
            groups[2].append((own, cy.at[here], recvy.at[slot, here], s1.at[2, j, k], r1.at[2, j, slot], device))
        for group in groups:
            moves += group
    for k in (3, 2, 1, 0):
        hd, ld = h ^ (k // 2), l ^ (k % 2)
        own = None if k else (c == l)
        moves.append((own, th, thr.at[lev], sth.at[k], rth.at[lev], (2 * sb + ld, 2 * hd + l)))
    for move in moves:
        start(*move)

    weights_copy.wait()

    col_id = lax.broadcasted_iota(jnp.int32, (8, LANES), 1)
    keep = jnp.where(has_low, 1.0, 0.0)

    def shifted(values, steps):
        return merged([pltpu.roll(v, (-steps) % LANES, 1) for v in values], steps)

    def merged(turned, steps):
        count = len(turned)
        if steps < 0:
            return [jnp.where(col_id < -steps, turned[m - 1], turned[m]) for m in range(count)]
        return [jnp.where(col_id >= LANES - steps, turned[(m + 1) % count], turned[m]) for m in range(count)]

    def unpack(j, source, target, twice):
        def do(i, _):
            for band in range(2):
                r0 = place(band, j)
                for pair in range(2):
                    for a in range(2):
                        for f in range(2):
                            line = pl.ds(r0 * pitch + 2 * i + a, CHUNK, stride=pitch)
                            ref = source.at[2 * band + pair] if twice else source.at[2 * band + pair, f]
                            target[i, pl.ds(8 * (band * rows + r0) + 4 * f + 2 * pair + a, CHUNK, stride=8), :] = ref[line, :]
            return 0
        lax.fori_loop(0, tiles, do, 0)

    def both_places(j):
        return [place(0, j), rows + place(1, j)]

    def at_row(row):
        return pl.ds(8 * row if isinstance(row, int) else pl.multiple_of(8 * row, 8), 8)

    def zonal_weights(j):
        def do(d, _):
            for first in both_places(j):
                at8 = at_row(first + d)
                cxs = [cxt[m, at8, :] for m in range(tiles)]
                for m, (cxr, cxe) in enumerate(zip(cxs, shifted(cxs, 1))):
                    west, east = stencil_weights(cxr), stencil_weights(cxe)
                    wz[0, m, at8, :] = west[0]
                    for n in range(1, 6):
                        w = west[n] - east[n - 1]
                        wz[n, m, at8, :] = w + 1.0 if n == 3 else w
                    wz[6, m, at8, :] = -east[5]
            return 0
        lax.fori_loop(0, CHUNK, do, 0)

    def meridional_weights(j):
        def do(i, _):
            for first in both_places(j):
                for d in range(CHUNK):
                    at8 = at_row(first + d)
                    cyr = cyt[i, at8, :]
                    if first + d == 0:
                        cyr = keep * cyr
                        cyrow[i] = cyr
                    for n, w in enumerate(face_weights(cyr)):
                        wy[n, i, at8, :] = w
            return 0
        lax.fori_loop(0, tiles, do, 0)

    def low_row():
        return copy_to(cyrow, cytop, sc, rc, (lat - 2, lev))

    def zonal(t, rows_here):
        f = [[field[t, m, at_row(row), :] for m in range(tiles)] for row in rows_here]
        flat = jnp.concatenate([v for one in f for v in one], axis=0)
        head = flat.astype(jnp.bfloat16)
        rest = (flat - head.astype(jnp.float32)).astype(jnp.bfloat16)
        parts = jnp.concatenate([head, rest], axis=1)
        turned = {}
        for n in range(0, len(SHIFTS), 2):
            moved = jnp.dot(parts, turns[:, n * LANES:(n + 2) * LANES], preferred_element_type=jnp.float32)
            turned[SHIFTS[n]], turned[SHIFTS[n + 1]] = moved[:, :LANES], moved[:, LANES:]
        for n, row in enumerate(rows_here):
            at8 = at_row(row)
            total = [wz[3, m, at8, :] * f[n][m] for m in range(tiles)]
            for k in (0, 1, 2, 4, 5, 6):
                steps = k - 3
                if steps in turned:
                    first = 8 * tiles * n
                    moved = merged([turned[steps][first + 8 * m:first + 8 * m + 8] for m in range(tiles)], steps)
                else:
                    moved = shifted(f[n], steps)
                total = [total[m] + wz[k, m, at8, :] * moved[m] for m in range(tiles)]
            to8 = at_row(row + HALO)
            for m in range(tiles):
                zon[t, m, to8, :] = total[m]

    def meridional(t, starts, n):
        def do(i, _):
            for r0 in starts:
                def z(row):
                    return zon[t, i, 8 * (row + HALO):8 * (row + HALO) + 8, :]

                window = [z(r0 + d) for d in range(-3, 3)]
                sums = [window[m] + window[m + 1] for m in range(5)]

                def face(m):
                    return 8.0 * sums[m] - (sums[m - 1] + sums[m + 1])
                values = [face(1), face(2), face(3)]
                before = None
                for row in range(r0, r0 + n + 1):
                    at8 = at_row(row)
                    p, q, r = wy[0, i, at8, :], wy[1, i, at8, :], wy[2, i, at8, :]
                    pos = p > 0.0
                    flux = p * values[1] - q * jnp.where(pos, values[0], values[2]) + r * jnp.where(
                        pos, window[2], window[3])
                    if before is not None:
                        field[t + 1, i, at_row(row - 1), :] = window[2] - (flux - before)
                    before = flux
                    if row < r0 + n:
                        window = window[1:] + [z(row + 3)]
                        sums = sums[1:] + [window[4] + window[5]]
                        values = values[1:] + [face(3)]
            return 0
        lax.fori_loop(0, tiles, do, 0, unroll=True)

    edge = 8 * HALO
    top = 8 * both
    ends = [0, both - HALO]

    def to_low(t):
        return copy_to(zon.at[t, :, pl.ds(edge, edge)], zon.at[t, :, pl.ds(edge + top, edge)],
                       sh.at[t, 0], rh.at[t, 0], (lat - 2, lev))

    def to_up(t):
        return copy_to(zon.at[t, :, pl.ds(top, edge)], zon.at[t, :, pl.ds(0, edge)],
                       sh.at[t, 1], rh.at[t, 1], (lat + 2, lev))

    def send_halo(t):
        zonal(t, [first + d for first in ends for d in range(HALO)])

        @pl.when(has_low)
        def _():
            to_low(t).start()

        @pl.when(has_up)
        def _():
            to_up(t).start()

    def wait_halo(t):
        @pl.when(has_low)
        def _():
            to_up(t).wait_recv()

        @pl.when(has_up)
        def _():
            to_low(t).wait_recv()

    def take_fields(j):
        for kind, ref in ((0, recvf), (1, recvx)):
            for s in range(4):
                for band in range(2):
                    if s // 2 == band:
                        here = span_of(band, j)
                        arrived(ref.at[s, :, here] if kind == 0 else ref.at[s, here], r1.at[kind, j, s])
        unpack(j, recvx, cxt, True)
        unpack(j, recvf, field.at[0], False)
        zonal_weights(j)

    def take_courant(j):
        for s in range(4):
            arrived(recvy.at[s, span_of(s // 2, j)], r1.at[2, j, s])
        unpack(j, recvy, cyt, True)
        meridional_weights(j)

    part = 8 * CHUNK

    def swap(j):
        theirs = pl.multiple_of(8 * ((1 - c) * rows + place(1 - c, j)), part)
        return copy_to(field.at[SUBSTEPS, :, pl.ds(theirs, part)], col.at[c, j], sx.at[j], rx.at[j], (lat, lev ^ 1))

    def send_swap(j):
        swap(j).start()
        ours = pl.multiple_of(8 * (c * rows + place(c, j)), part)
        col[c, j] = field[SUBSTEPS, :, pl.ds(ours, part), :]

    full = (8, LANES)

    def take_thickness():
        for s in range(4):
            arrived(thr.at[s], rth.at[s])

        def do(i, _):
            for j in range(chunks):
                first = place(c, j) * pitch + 2 * i
                for k in range(8):
                    piece = thr[k // 2, pl.ds(first + k % 2, CHUNK, stride=pitch), :]
                    for f in range(2):
                        tht[j, i, pl.ds(8 * k + f, CHUNK, stride=2), :] = piece
            return 0
        lax.fori_loop(0, tiles, do, 0)

    def columns(j, i):
        weights = [jnp.full(full, wts[k], jnp.float32) for k in range(8)]
        whole = weights[0]
        for k in range(1, 8):
            whole = whole + weights[k]
        inverse = 1.0 / whole
        thick = [tht[j, i, 8 * k:8 * k + 8, :] for k in range(8)]
        bounds = [jnp.full(full, TOP_PRESSURE, jnp.float32)]
        for k in range(8):
            bounds.append(bounds[-1] + thick[k])
        span = bounds[8] - TOP_PRESSURE
        low, up, total = [], [], None
        for k in range(8):
            total = weights[k] if total is None else total + weights[k]
            low.append(TOP_PRESSURE + span * (total * inverse))
            up.append(low[k] - span * (weights[k] * inverse))
        return thick, bounds, low, up

    def remap(j):
        def do(i, _):
            thick, bounds, low, up = columns(j, i)
            density = [col[k // 4, j, i, pl.ds(k % 4, 8, stride=4), :] / thick[k] for k in range(8)]
            for k in range(8):
                total = None
                for n in range(8):
                    cut = jnp.maximum(0.0, jnp.minimum(bounds[n + 1], low[k]) - jnp.maximum(bounds[n], up[k]))
                    total = density[n] * cut if total is None else total + density[n] * cut
                tmp[i, 8 * k:8 * k + 8, :] = total
            for k in range(8):
                for f in range(2):
                    outp[k // 2, j, f, pl.ds(2 * i + k % 2, CHUNK, stride=pitch), :] = (
                        tmp[i, pl.ds(8 * k + f, CHUNK, stride=2), :])
            return 0
        lax.fori_loop(0, tiles, do, 0)

    def integrate(j):
        def do(i, _):
            _, _, low, up = columns(j, i)
            total = None
            for k in range(7, -1, -1):
                layer = GAS_FACTOR * tmp[i, 8 * k:8 * k + 8, :] / (low[k] - up[k]) * jnp.log(low[k] / up[k])
                total = layer if total is None else total + layer
                tmp[i, 8 * k:8 * k + 8, :] = total
            for k in range(8):
                geop[k // 2, j, pl.ds(2 * i + k % 2, CHUNK, stride=pitch), :] = (
                    tmp[i, pl.ds(8 * k, CHUNK, stride=2), :])
            return 0
        lax.fori_loop(0, tiles, do, 0)

    def result_moves(j):
        here = span_of(c, j)
        for k in (3, 2, 1, 0):
            gd = lev ^ k
            yield (None if k else (c == l), outp.at[gd, j], out.at[pl.ds(2 * y, 2), here],
                   so.at[j, k], ro.at[j, y], (2 * sb + c, gd))

    def integral_moves(j):
        here = span_of(c, j)
        for k in (3, 2, 1, 0):
            gd = lev ^ k
            yield (None if k else (c == l), geop.at[gd, j], geor.at[here], sg.at[j, k], rg.at[j], (2 * sb + c, gd))

    def send_results(j):
        swap(j).wait_recv()
        remap(j)
        for move in result_moves(j):
            start(*move)

        @pl.when(y == 0)
        def _():
            integrate(j)
            for move in integral_moves(j):
                start(*move)

    take_fields(0)
    send_halo(0)
    zonal(0, [HALO, both - HALO - 1])
    take_courant(0)

    @pl.when(has_low)
    def _():
        low_row().start()

    take_fields(1)
    zonal(0, [first + d for first in both_places(1) for d in range(CHUNK)])
    take_courant(1)

    @pl.when(has_up)
    def _():
        low_row().wait_recv()
    for n, w in enumerate(face_weights(cytop[...])):
        wy[n, :, top:top + 8, :] = w
    wait_halo(0)
    meridional(0, [0, both - 5], 5)
    send_halo(1)
    zonal(1, [3, 4, both - 5, both - 4])

    take_fields(2)
    zonal(0, list(range(8, 16)))
    take_courant(2)
    meridional(0, [5], both - 10)
    zonal(1, list(range(5, 19)))
    wait_halo(1)
    meridional(1, ends, HALO)
    send_halo(2)
    meridional(1, [HALO], both - 2 * HALO)
    zonal(2, list(range(3, 13)))
    zonal(2, list(range(13, 21)))
    meridional(2, [5], both - 10)
    zonal(3, list(range(5, 19)))
    meridional(3, [8], 8)
    send_swap(2)

    wait_halo(2)
    meridional(2, ends, HALO)
    send_halo(3)
    take_thickness()
    send_results(2)
    meridional(2, [HALO, both - 5], 2)
    zonal(3, [3, 4, both - 5, both - 4])
    meridional(3, [HALO, both - 8], 5)
    send_swap(1)
    send_results(1)

    wait_halo(3)
    meridional(3, ends, HALO)
    send_swap(0)
    send_results(0)

    for j in range(chunks):
        arrived(geor.at[span_of(l, j)], rg.at[j])
    for j in range(chunks):
        for s in range(4):
            arrived(out.at[pl.ds(2 * s, 2), span_of(l, j)], ro.at[j, s])

    for move in moves:
        sent(*move)
    for j in range(chunks):
        swap(j).wait_send()
        for move in result_moves(j):
            sent(*move)

    @pl.when(y == 0)
    def _():
        for j in range(chunks):
            for move in integral_moves(j):
                sent(*move)

    @pl.when(has_low)
    def _():
        low_row().wait_send()
        for t in range(SUBSTEPS):
            to_low(t).wait_send()

    @pl.when(has_up)
    def _():
        for t in range(SUBSTEPS):
            to_up(t).wait_send()


def finish(rows, tiles, result, integral, surface, out, geo, held, total, sgeo, sems, gsems):
    loads = [pltpu.make_async_copy(integral, total, gsems.at[0]), pltpu.make_async_copy(surface, sgeo, gsems.at[1])]
    takes = [pltpu.make_async_copy(result.at[f], held.at[f], sems.at[0, f]) for f in range(8)]
    gives = [pltpu.make_async_copy(held.at[f], out.at[f], sems.at[1, f]) for f in range(8)]
    for copy in loads + takes:
        copy.start()
    for copy in loads:
        copy.wait()
    pitch = 2 * tiles
    for i in range(tiles):
        for r0, n in ((0, 8), (8, rows - 8)):
            piece = sgeo[r0:r0 + n, i * LANES:(i + 1) * LANES]
            for a in range(2):
                here = pl.ds(r0 * pitch + 2 * i + a, n, stride=pitch)
                total[here, :] = total[here, :] + piece
    store = pltpu.make_async_copy(total, geo, gsems.at[2])
    store.start()
    for take, give in zip(takes, gives):
        take.wait()
        give.start()
    for copy in gives + [store]:
        copy.wait()


def in_lines(array):
    lead = array.ndim - 3
    levels, rows, nlon = array.shape[lead:]
    tiles = nlon // LANES
    split = array.reshape(array.shape[:-1] + (tiles, LANES))
    order = tuple(range(lead)) + (lead + 1, lead + 2, lead, lead + 3)
    split = with_layout_constraint(split, Layout(major_to_minor=order))
    return jnp.transpose(split, order).reshape(array.shape[:lead] + (rows * tiles * levels, LANES))


def from_lines(array, levels, rows):
    lead = array.ndim - 2
    tiles = array.shape[-2] // (levels * rows)
    split = array.reshape(array.shape[:lead] + (rows, tiles, levels, LANES))
    split = jnp.transpose(split, tuple(range(lead)) + (lead + 2, lead, lead + 1, lead + 3))
    order = tuple(range(lead)) + (lead + 1, lead + 2, lead, lead + 3)
    split = with_layout_constraint(split, Layout(major_to_minor=order))
    return split.reshape(array.shape[:lead] + (levels, rows, tiles * LANES))


def body(nsuper, tracers, courant_x, courant_y, thickness, level_weights, surface_geo):
    levels, rows, nlon = thickness.shape
    tiles = nlon // LANES
    f32 = jnp.float32
    hbm = pl.BlockSpec(memory_space=pltpu.HBM)
    both = 2 * rows
    lines = rows * tiles * levels
    chunks = rows // CHUNK

    def buffer(*shape):
        return pltpu.VMEM(shape + (LANES,), f32)

    dma = pltpu.SemaphoreType.DMA
    scratch = [
        pltpu.SMEM((8,), f32), dma,
        buffer(4, 2, lines), buffer(4, lines), buffer(4, lines), buffer(4, lines),
        buffer(SUBSTEPS + 1, tiles, 8 * both), buffer(SUBSTEPS, tiles, 8 * (both + 2 * HALO)),
        buffer(tiles, 8 * both), buffer(tiles, 8 * both),
        buffer(7, tiles, 8 * both), buffer(3, tiles, 8 * (both + 1)),
        buffer(tiles, 8), buffer(tiles, 8), buffer(chunks, tiles, 64),
        buffer(2, chunks, tiles, 8 * CHUNK), buffer(tiles, 64),
        buffer(4, chunks, 2, lines // chunks), buffer(4, chunks, lines // chunks),
        pltpu.VMEM((2 * LANES, len(SHIFTS) * LANES), jnp.bfloat16),
        dma((3, chunks, 4)), dma((3, chunks, 4)), dma((4,)), dma((4,)), dma((SUBSTEPS, 2)), dma((SUBSTEPS, 2)),
        dma, dma, dma((chunks,)), dma((chunks,)),
        dma((chunks, 4)), dma((chunks, 4)), dma((chunks, 4)), dma((chunks,)),
    ]
    result, integral = pl.pallas_call(
        functools.partial(kernel, nsuper, rows, tiles),
        out_shape=(jax.ShapeDtypeStruct((8, lines, LANES), f32), jax.ShapeDtypeStruct((lines, LANES), f32)),
        in_specs=[hbm] * 5,
        out_specs=(hbm, hbm),
        scratch_shapes=scratch,
        compiler_params=pltpu.CompilerParams(
            collective_id=0, has_side_effects=True, vmem_limit_bytes=60 * 2**20),
        name="transport_remap",
    )(in_lines(tracers), in_lines(courant_x), in_lines(courant_y), in_lines(thickness), level_weights)
    out, geo = pl.pallas_call(
        functools.partial(finish, rows, tiles),
        out_shape=(jax.ShapeDtypeStruct((8, lines, LANES), f32), jax.ShapeDtypeStruct((lines, LANES), f32)),
        in_specs=[hbm] * 3,
        out_specs=(hbm, hbm),
        scratch_shapes=[buffer(8, lines), buffer(lines), pltpu.VMEM((rows, nlon), f32), dma((2, 8)), dma((3,))],
        compiler_params=pltpu.CompilerParams(vmem_limit_bytes=60 * 2**20),
        name="finish",
    )(result, integral, surface_geo)
    return from_lines(out, levels, rows), from_lines(geo, levels, rows)


def solution(mesh):
    in_specs = (
        P(None, "lev", "lat", None),
        P("lev", "lat", None),
        P("lev", "lat", None),
        P("lev", "lat", None),
        P(),
        P("lat", None),
    )
    out_specs = (P(None, "lev", "lat", None), P("lev", "lat", None))
    run = functools.partial(body, mesh.shape["lat"] // 2)
    return jax.shard_map(run, mesh=mesh, in_specs=in_specs, out_specs=out_specs, check_vma=False)
```

```python
import functools

import jax
import jax.numpy as jnp
from jax import lax
from jax.experimental import pallas as pl
from jax.experimental.layout import Layout, with_layout_constraint
from jax.experimental.pallas import tpu as pltpu
from jax.sharding import PartitionSpec as P

SUBSTEPS = 4
HALO = 3
CHUNK = 4
LANES = 128
TOP_PRESSURE = 1.0
GAS_FACTOR = 0.3
SHIFTS = (-3, -2, 2, 3)


def face_weights(courant):
    size = jnp.abs(courant)
    rest = 1.0 - size
    scaled = courant * rest * (1.0 / 12.0)
    return scaled * rest, scaled * size, courant * size * (3.0 - 2.0 * size)


def stencil_weights(courant):
    p, q, r = face_weights(courant)
    pos = courant > 0.0
    qp, rp = jnp.where(pos, q, 0.0), jnp.where(pos, r, 0.0)
    qn, rn = q - qp, r - rp
    p7 = 7.0 * p
    return [
        qp,
        -p - 7.0 * qp,
        p7 - 7.0 * qp + qn + rp,
        p7 + qp - 7.0 * qn + rn,
        -p - 7.0 * qn,
        qn,
    ]


def kernel(nsuper, rows, tiles, tr, cx, cy, th, wts_hbm, out, above, span_out, wts, lsem, spans,
           recvf, recvx, recvy, thr, field, zon, cxt, cyt, wz, wy, cyrow, cytop, tht, col, tmp, outp, geop, turns,
           s1, r1, sth, rth, sh, rh, sc, rc, sx, rx, so, ro, sg, rg, sp):
    lat, lev = lax.axis_index("lat"), lax.axis_index("lev")
    sb, l = lat // 2, lat % 2
    h, c = lev // 2, lev % 2
    y = 2 * h + l
    both = 2 * rows
    chunks = rows // CHUNK
    pitch = 2 * tiles
    lines = CHUNK * pitch
    has_low, has_up = sb > 0, sb < nsuper - 1

    weights_copy = pltpu.make_async_copy(wts_hbm, wts, lsem)
    weights_copy.start()

    barrier = pltpu.get_barrier_semaphore()
    for k in range(1, 8):
        pl.semaphore_signal(barrier, 1, device_id=(2 * sb + (l ^ (k // 4)), lev ^ (k % 4)))

    @pl.when(has_low)
    def _():
        pl.semaphore_signal(barrier, 1, device_id=(lat - 2, lev))

    @pl.when(has_up)
    def _():
        pl.semaphore_signal(barrier, 1, device_id=(lat + 2, lev))

    @pl.when(jnp.logical_not(has_low))
    def _():
        for t in range(SUBSTEPS):
            zon[t, :, 0:8 * HALO, :] = jnp.zeros((tiles, 8 * HALO, LANES), jnp.float32)

    @pl.when(jnp.logical_not(has_up))
    def _():
        for t in range(SUBSTEPS):
            zon[t, :, 8 * (HALO + both):, :] = jnp.zeros((tiles, 8 * HALO, LANES), jnp.float32)
        cytop[...] = jnp.zeros((tiles, 8, LANES), jnp.float32)

    source = lax.broadcasted_iota(jnp.int32, (2 * LANES, LANES), 0) % LANES
    target = lax.broadcasted_iota(jnp.int32, (2 * LANES, LANES), 1)
    for n, steps in enumerate(SHIFTS):
        turns[:, n * LANES:(n + 1) * LANES] = jnp.where(
            source == (target + (steps + LANES)) % LANES, 1.0, 0.0).astype(jnp.bfloat16)

    others = 7 + has_low.astype(jnp.int32) + has_up.astype(jnp.int32)
    pl.semaphore_wait(barrier, others)

    def copy_to(src, dst, ssem, rsem, device):
        return pltpu.make_async_remote_copy(src, dst, ssem, rsem, device_id=device)

    def start(own, src, dst, ssem, rsem, device):
        if own is None:
            copy_to(src, dst, ssem, rsem, device).start()
            return

        @pl.when(own)
        def _():
            pltpu.make_async_copy(src, dst, rsem).start()

        @pl.when(jnp.logical_not(own))
        def _():
            copy_to(src, dst, ssem, rsem, device).start()

    def sent(own, src, dst, ssem, rsem, device):
        if own is None:
            copy_to(src, dst, ssem, rsem, device).wait_send()
            return

        @pl.when(jnp.logical_not(own))
        def _():
            copy_to(src, dst, ssem, rsem, device).wait_send()

    def arrived(dst, rsem):
        pltpu.make_async_copy(dst, dst, rsem).wait()

    def place(band, j):
        if isinstance(band, int):
            return j * CHUNK if band == 0 else rows - (j + 1) * CHUNK
        return jnp.where(band == 0, j * CHUNK, rows - (j + 1) * CHUNK)

    def span_of(band, j):
        first = place(band, j) * pitch
        return pl.ds(first if isinstance(first, int) else pl.multiple_of(first, 8), lines)

    moves = []
    slot = 2 * l + c
    for j in range(chunks):
        here = span_of(l, j)
        groups = [[], [], []]
        for k in (3, 2, 1, 0):
            hd, ld = h ^ (k // 2), l ^ (k % 2)
            own = None if k else (c == h)
            device = (2 * sb + ld, 2 * hd + h)
            groups[0].append((own, tr.at[pl.ds(2 * (2 * hd + ld), 2), here], recvf.at[slot, :, here],
                              s1.at[0, j, k], r1.at[0, j, slot], device))
            groups[1].append((own, cx.at[here], recvx.at[slot, here], s1.at[1, j, k], r1.at[1, j, slot], device))
            groups[2].append((own, cy.at[here], recvy.at[slot, here], s1.at[2, j, k], r1.at[2, j, slot], device))
        for group in groups:
            moves += group
    for k in (3, 2, 1, 0):
        hd, ld = h ^ (k // 2), l ^ (k % 2)
        own = None if k else (c == l)
        moves.append((own, th, thr.at[lev], sth.at[k], rth.at[lev], (2 * sb + ld, 2 * hd + l)))
    for move in moves:
        start(*move)

    weights_copy.wait()

    col_id = lax.broadcasted_iota(jnp.int32, (8, LANES), 1)
    keep = jnp.where(has_low, 1.0, 0.0)

    def shifted(values, steps):
        return merged([pltpu.roll(v, (-steps) % LANES, 1) for v in values], steps)

    def merged(turned, steps):
        count = len(turned)
        if steps < 0:
            return [jnp.where(col_id < -steps, turned[m - 1], turned[m]) for m in range(count)]
        return [jnp.where(col_id >= LANES - steps, turned[(m + 1) % count], turned[m]) for m in range(count)]

    def unpack(j, source, target, twice):
        def do(i, _):
            for band in range(2):
                r0 = place(band, j)
                for pair in range(2):
                    for a in range(2):
                        for f in range(2):
                            line = pl.ds(r0 * pitch + 2 * i + a, CHUNK, stride=pitch)
                            ref = source.at[2 * band + pair] if twice else source.at[2 * band + pair, f]
                            target[i, pl.ds(8 * (band * rows + r0) + 4 * f + 2 * pair + a, CHUNK, stride=8), :] = ref[line, :]
            return 0
        lax.fori_loop(0, tiles, do, 0)

    def both_places(j):
        return [place(0, j), rows + place(1, j)]

    def at_row(row):
        return pl.ds(8 * row if isinstance(row, int) else pl.multiple_of(8 * row, 8), 8)

    def zonal_weights(j):
        def do(d, _):
            for first in both_places(j):
                at8 = at_row(first + d)
                cxs = [cxt[m, at8, :] for m in range(tiles)]
                for m, (cxr, cxe) in enumerate(zip(cxs, shifted(cxs, 1))):
                    west, east = stencil_weights(cxr), stencil_weights(cxe)
                    wz[0, m, at8, :] = west[0]
                    for n in range(1, 6):
                        w = west[n] - east[n - 1]
                        wz[n, m, at8, :] = w + 1.0 if n == 3 else w
                    wz[6, m, at8, :] = -east[5]
            return 0
        lax.fori_loop(0, CHUNK, do, 0)

    def meridional_weights(j):
        def do(i, _):
            for first in both_places(j):
                for d in range(CHUNK):
                    at8 = at_row(first + d)
                    cyr = cyt[i, at8, :]
                    if first + d == 0:
                        cyr = keep * cyr
                        cyrow[i] = cyr
                    for n, w in enumerate(face_weights(cyr)):
                        wy[n, i, at8, :] = w
            return 0
        lax.fori_loop(0, tiles, do, 0)

    def low_row():
        return copy_to(cyrow, cytop, sc, rc, (lat - 2, lev))

    def zonal(t, rows_here):
        f = [[field[t, m, at_row(row), :] for m in range(tiles)] for row in rows_here]
        flat = jnp.concatenate([v for one in f for v in one], axis=0)
        head = flat.astype(jnp.bfloat16)
        rest = (flat - head.astype(jnp.float32)).astype(jnp.bfloat16)
        parts = jnp.concatenate([head, rest], axis=1)
        turned = {}
        for n in range(0, len(SHIFTS), 2):
            moved = jnp.dot(parts, turns[:, n * LANES:(n + 2) * LANES], preferred_element_type=jnp.float32)
            turned[SHIFTS[n]], turned[SHIFTS[n + 1]] = moved[:, :LANES], moved[:, LANES:]
        for n, row in enumerate(rows_here):
            at8 = at_row(row)
            total = [wz[3, m, at8, :] * f[n][m] for m in range(tiles)]
            for k in (0, 1, 2, 4, 5, 6):
                steps = k - 3
                if steps in turned:
                    first = 8 * tiles * n
                    moved = merged([turned[steps][first + 8 * m:first + 8 * m + 8] for m in range(tiles)], steps)
                else:
                    moved = shifted(f[n], steps)
                total = [total[m] + wz[k, m, at8, :] * moved[m] for m in range(tiles)]
            to8 = at_row(row + HALO)
            for m in range(tiles):
                zon[t, m, to8, :] = total[m]

    def meridional(t, starts, n):
        def do(i, _):
            for r0 in starts:
                def z(row):
                    return zon[t, i, 8 * (row + HALO):8 * (row + HALO) + 8, :]

                window = [z(r0 + d) for d in range(-3, 3)]
                sums = [window[m] + window[m + 1] for m in range(5)]

                def face(m):
                    return 8.0 * sums[m] - (sums[m - 1] + sums[m + 1])
                values = [face(1), face(2), face(3)]
                before = None
                for row in range(r0, r0 + n + 1):
                    at8 = at_row(row)
                    p, q, r = wy[0, i, at8, :], wy[1, i, at8, :], wy[2, i, at8, :]
                    pos = p > 0.0
                    flux = p * values[1] - q * jnp.where(pos, values[0], values[2]) + r * jnp.where(
                        pos, window[2], window[3])
                    if before is not None:
                        field[t + 1, i, at_row(row - 1), :] = window[2] - (flux - before)
                    before = flux
                    if row < r0 + n:
                        window = window[1:] + [z(row + 3)]
                        sums = sums[1:] + [window[4] + window[5]]
                        values = values[1:] + [face(3)]
            return 0
        lax.fori_loop(0, tiles, do, 0, unroll=True)

    edge = 8 * HALO
    top = 8 * both
    ends = [0, both - HALO]

    def to_low(t):
        return copy_to(zon.at[t, :, pl.ds(edge, edge)], zon.at[t, :, pl.ds(edge + top, edge)],
                       sh.at[t, 0], rh.at[t, 0], (lat - 2, lev))

    def to_up(t):
        return copy_to(zon.at[t, :, pl.ds(top, edge)], zon.at[t, :, pl.ds(0, edge)],
                       sh.at[t, 1], rh.at[t, 1], (lat + 2, lev))

    def send_halo(t):
        zonal(t, [first + d for first in ends for d in range(HALO)])

        @pl.when(has_low)
        def _():
            to_low(t).start()

        @pl.when(has_up)
        def _():
            to_up(t).start()

    def wait_halo(t):
        @pl.when(has_low)
        def _():
            to_up(t).wait_recv()

        @pl.when(has_up)
        def _():
            to_low(t).wait_recv()

    def take_fields(j):
        for kind, ref in ((0, recvf), (1, recvx)):
            for s in range(4):
                for band in range(2):
                    if s // 2 == band:
                        here = span_of(band, j)
                        arrived(ref.at[s, :, here] if kind == 0 else ref.at[s, here], r1.at[kind, j, s])
        unpack(j, recvx, cxt, True)
        unpack(j, recvf, field.at[0], False)
        zonal_weights(j)

    def take_courant(j):
        for s in range(4):
            arrived(recvy.at[s, span_of(s // 2, j)], r1.at[2, j, s])
        unpack(j, recvy, cyt, True)
        meridional_weights(j)

    part = 8 * CHUNK

    def swap(j):
        theirs = pl.multiple_of(8 * ((1 - c) * rows + place(1 - c, j)), part)
        return copy_to(field.at[SUBSTEPS, :, pl.ds(theirs, part)], col.at[c, j], sx.at[j], rx.at[j], (lat, lev ^ 1))

    def send_swap(j):
        swap(j).start()
        ours = pl.multiple_of(8 * (c * rows + place(c, j)), part)
        col[c, j] = field[SUBSTEPS, :, pl.ds(ours, part), :]

    full = (8, LANES)

    def take_thickness():
        for s in range(4):
            arrived(thr.at[s], rth.at[s])

        def do(i, _):
            for j in range(chunks):
                first = place(c, j) * pitch + 2 * i
                for k in range(8):
                    piece = thr[k // 2, pl.ds(first + k % 2, CHUNK, stride=pitch), :]
                    for f in range(2):
                        tht[j, i, pl.ds(8 * k + f, CHUNK, stride=2), :] = piece
            for r0, n in ((0, 8), (8, rows - 8)):
                total = None
                for k in range(8):
                    piece = thr[k // 2, pl.ds(r0 * pitch + 2 * i + k % 2, n, stride=pitch), :]
                    total = piece if total is None else total + piece
                spans[pl.ds(r0 * tiles + i, n, stride=tiles), :] = total
            return 0
        lax.fori_loop(0, tiles, do, 0)

        @pl.when(c == l)
        def _():
            keep_spans.start()
            give_spans.start()

    keep_spans = pltpu.make_async_copy(spans, span_out, sp.at[0])
    give_spans = copy_to(spans, span_out, sp.at[1], sp.at[2], (lat, lev ^ 1))

    def columns(j, i):
        weights = [jnp.full(full, wts[k], jnp.float32) for k in range(8)]
        whole = weights[0]
        for k in range(1, 8):
            whole = whole + weights[k]
        inverse = 1.0 / whole
        thick = [tht[j, i, 8 * k:8 * k + 8, :] for k in range(8)]
        bounds = [jnp.full(full, TOP_PRESSURE, jnp.float32)]
        for k in range(8):
            bounds.append(bounds[-1] + thick[k])
        span = bounds[8] - TOP_PRESSURE
        low, up, total = [], [], None
        for k in range(8):
            total = weights[k] if total is None else total + weights[k]
            low.append(TOP_PRESSURE + span * (total * inverse))
            up.append(low[k] - span * (weights[k] * inverse))
        return thick, bounds, low, up

    def remap(j):
        def do(i, _):
            thick, bounds, low, up = columns(j, i)
            density = [col[k // 4, j, i, pl.ds(k % 4, 8, stride=4), :] / thick[k] for k in range(8)]
            for k in range(8):
                total = None
                for n in range(8):
                    cut = jnp.maximum(0.0, jnp.minimum(bounds[n + 1], low[k]) - jnp.maximum(bounds[n], up[k]))
                    total = density[n] * cut if total is None else total + density[n] * cut
                tmp[j, i, 8 * k:8 * k + 8, :] = total
            for k in range(8):
                for f in range(2):
                    outp[k // 2, j, f, pl.ds(2 * i + k % 2, CHUNK, stride=pitch), :] = (
                        tmp[j, i, pl.ds(8 * k + f, CHUNK, stride=2), :])
            return 0
        lax.fori_loop(0, tiles, do, 0)

    def integrate(j):
        def do(i, _):
            _, _, low, up = columns(j, i)
            total = None
            for k in range(7, -1, -1):
                layer = GAS_FACTOR * tmp[j, i, 8 * k:8 * k + 8, :] / (low[k] - up[k]) * jnp.log(low[k] / up[k])
                total = layer if total is None else total + layer
                tmp[j, i, 8 * k:8 * k + 8, :] = total
            for n in range(3):
                geop[n, j, pl.ds(i, CHUNK, stride=tiles), :] = tmp[j, i, pl.ds(8 * (2 * n + 2), CHUNK, stride=2), :]
            return 0
        lax.fori_loop(0, tiles, do, 0)

    def result_moves(j):
        here = span_of(c, j)
        for k in (3, 2, 1, 0):
            gd = lev ^ k
            yield (None if k else (c == l), outp.at[gd, j], out.at[pl.ds(2 * y, 2), here],
                   so.at[j, k], ro.at[j, y], (2 * sb + c, gd))

    def integral_moves(j):
        for n in range(3):
            yield (None if n else (c == 0), geop.at[n, j], above.at[j], sg.at[j, n], rg.at[j], (2 * sb + c, n))

    def send_results(j):
        swap(j).wait_recv()
        remap(j)
        for move in result_moves(j):
            start(*move)

    def send_integrals(*which):
        @pl.when(y == 0)
        def _():
            for j in which:
                integrate(j)
                for move in integral_moves(j):
                    start(*move)

    take_fields(0)
    send_halo(0)
    zonal(0, [HALO, both - HALO - 1])
    take_courant(0)

    @pl.when(has_low)
    def _():
        low_row().start()

    take_fields(1)
    zonal(0, [first + d for first in both_places(1) for d in range(CHUNK)])
    take_courant(1)

    @pl.when(has_up)
    def _():
        low_row().wait_recv()
    for n, w in enumerate(face_weights(cytop[...])):
        wy[n, :, top:top + 8, :] = w
    wait_halo(0)
    meridional(0, [0, both - 5], 5)
    send_halo(1)
    zonal(1, [3, 4, both - 5, both - 4])

    take_fields(2)
    zonal(0, list(range(8, 16)))
    take_courant(2)
    meridional(0, [5], both - 10)
    zonal(1, list(range(5, 19)))
    wait_halo(1)
    meridional(1, ends, HALO)
    send_halo(2)
    meridional(1, [HALO], both - 2 * HALO)
    zonal(2, list(range(3, 13)))
    zonal(2, list(range(13, 21)))
    meridional(2, [5], both - 10)
    zonal(3, list(range(5, 19)))
    meridional(3, [8], 8)
    send_swap(2)

    take_thickness()

    wait_halo(2)
    meridional(2, ends, HALO)
    send_halo(3)
    send_results(2)
    meridional(2, [HALO, both - 5], 2)
    zonal(3, [3, 4, both - 5, both - 4])
    meridional(3, [HALO, both - 8], 5)
    send_swap(1)
    send_integrals(2)
    send_results(1)

    wait_halo(3)
    meridional(3, ends, HALO)
    send_swap(0)
    send_integrals(1)
    send_results(0)
    send_integrals(0)

    @pl.when(lev < 3)
    def _():
        for j in range(chunks):
            arrived(above.at[j], rg.at[j])

    @pl.when(c == l)
    def _():
        keep_spans.wait()
        give_spans.wait_send()

    @pl.when(c != l)
    def _():
        give_spans.wait_recv()
    for j in range(chunks):
        for s in range(4):
            arrived(out.at[pl.ds(2 * s, 2), span_of(l, j)], ro.at[j, s])

    for move in moves:
        sent(*move)
    for j in range(chunks):
        swap(j).wait_send()
        for move in result_moves(j):
            sent(*move)

    @pl.when(y == 0)
    def _():
        for j in range(chunks):
            for move in integral_moves(j):
                sent(*move)

    @pl.when(has_low)
    def _():
        low_row().wait_send()
        for t in range(SUBSTEPS):
            to_low(t).wait_send()

    @pl.when(has_up)
    def _():
        for t in range(SUBSTEPS):
            to_up(t).wait_send()


def finish(rows, tiles, result, above, span_in, wts, surface, out, geo, held, over, spans, sgeo, sums, total, sems, gsems):
    lat, lev = lax.axis_index("lat"), lax.axis_index("lev")
    l = lat % 2
    pitch = 2 * tiles
    loads = [pltpu.make_async_copy(above, over, gsems.at[0]), pltpu.make_async_copy(span_in, spans, gsems.at[1]),
             pltpu.make_async_copy(surface, sgeo, gsems.at[2])]
    takes = [pltpu.make_async_copy(result.at[f], held.at[f], sems.at[0, f]) for f in range(8)]
    gives = [pltpu.make_async_copy(held.at[f], out.at[f], sems.at[1, f]) for f in range(8)]
    for copy in takes[:1] + loads + takes[1:]:
        copy.start()
    for copy in loads:
        copy.wait()
    takes[0].wait()
    gives[0].start()
    for j in range(rows // CHUNK):
        row = jnp.where(l == 0, j * CHUNK, rows - (j + 1) * CHUNK)
        for i in range(tiles):
            sums[pl.ds(row * tiles + i, CHUNK, stride=tiles), :] = over[j, pl.ds(i, CHUNK, stride=tiles), :]
    for r0, n in ((0, 8), (8, rows - 8)):
        shape = (n, LANES)
        whole, below, mine = None, jnp.zeros(shape, jnp.float32), [None, None]
        for k in range(8):
            weight = jnp.full(shape, wts[k], jnp.float32)
            whole = weight if whole is None else whole + weight
            below = below + jnp.where(k < 2 * lev, weight, 0.0)
            mine[k % 2] = weight if k < 2 else jnp.where(k // 2 == lev, weight, mine[k % 2])
        inverse = 1.0 / whole
        shares = [mine[0] * inverse, mine[1] * inverse]
        fractions = [(below + mine[0]) * inverse, (below + mine[0] + mine[1]) * inverse]
        for i in range(tiles):
            span = spans[pl.ds(r0 * tiles + i, n, stride=tiles), :]
            value = jnp.where(lev < 3, sums[pl.ds(r0 * tiles + i, n, stride=tiles), :], 0.0)
            value = value + sgeo[r0:r0 + n, i * LANES:(i + 1) * LANES]
            for a in (1, 0):
                here = pl.ds(r0 * pitch + 2 * i + a, n, stride=pitch)
                low = TOP_PRESSURE + span * fractions[a]
                up = low - span * shares[a]
                value = value + GAS_FACTOR * held[0, here, :] / (low - up) * jnp.log(low / up)
                total[here, :] = value
    store = pltpu.make_async_copy(total, geo, gsems.at[3])
    store.start()
    for take, give in zip(takes[1:], gives[1:]):
        take.wait()
        give.start()
    for copy in gives + [store]:
        copy.wait()


def in_lines(array):
    lead = array.ndim - 3
    levels, rows, nlon = array.shape[lead:]
    tiles = nlon // LANES
    split = array.reshape(array.shape[:-1] + (tiles, LANES))
    order = tuple(range(lead)) + (lead + 1, lead + 2, lead, lead + 3)
    split = with_layout_constraint(split, Layout(major_to_minor=order))
    return jnp.transpose(split, order).reshape(array.shape[:lead] + (rows * tiles * levels, LANES))


def from_lines(array, levels, rows):
    lead = array.ndim - 2
    tiles = array.shape[-2] // (levels * rows)
    split = array.reshape(array.shape[:lead] + (rows, tiles, levels, LANES))
    split = jnp.transpose(split, tuple(range(lead)) + (lead + 2, lead, lead + 1, lead + 3))
    order = tuple(range(lead)) + (lead + 1, lead + 2, lead, lead + 3)
    split = with_layout_constraint(split, Layout(major_to_minor=order))
    return split.reshape(array.shape[:lead] + (levels, rows, tiles * LANES))


def body(nsuper, tracers, courant_x, courant_y, thickness, level_weights, surface_geo):
    levels, rows, nlon = thickness.shape
    tiles = nlon // LANES
    f32 = jnp.float32
    hbm = pl.BlockSpec(memory_space=pltpu.HBM)
    both = 2 * rows
    lines = rows * tiles * levels
    chunks = rows // CHUNK
    sum_lines = -(-CHUNK * tiles // 8) * 8
    span_lines = -(-rows * tiles // 8) * 8

    def buffer(*shape):
        return pltpu.VMEM(shape + (LANES,), f32)

    dma = pltpu.SemaphoreType.DMA
    scratch = [
        pltpu.SMEM((8,), f32), dma, buffer(span_lines),
        buffer(4, 2, lines), buffer(4, lines), buffer(4, lines), buffer(4, lines),
        buffer(SUBSTEPS + 1, tiles, 8 * both), buffer(SUBSTEPS, tiles, 8 * (both + 2 * HALO)),
        buffer(tiles, 8 * both), buffer(tiles, 8 * both),
        buffer(7, tiles, 8 * both), buffer(3, tiles, 8 * (both + 1)),
        buffer(tiles, 8), buffer(tiles, 8), buffer(chunks, tiles, 64),
        buffer(2, chunks, tiles, 8 * CHUNK), buffer(chunks, tiles, 64),
        buffer(4, chunks, 2, lines // chunks), buffer(3, chunks, sum_lines),
        pltpu.VMEM((2 * LANES, len(SHIFTS) * LANES), jnp.bfloat16),
        dma((3, chunks, 4)), dma((3, chunks, 4)), dma((4,)), dma((4,)), dma((SUBSTEPS, 2)), dma((SUBSTEPS, 2)),
        dma, dma, dma((chunks,)), dma((chunks,)),
        dma((chunks, 4)), dma((chunks, 4)), dma((chunks, 3)), dma((chunks,)), dma((3,)),
    ]
    results = jax.ShapeDtypeStruct((8, lines, LANES), f32)
    result, above, spans = pl.pallas_call(
        functools.partial(kernel, nsuper, rows, tiles),
        out_shape=(results, jax.ShapeDtypeStruct((chunks, sum_lines, LANES), f32),
                   jax.ShapeDtypeStruct((span_lines, LANES), f32)),
        in_specs=[hbm] * 5,
        out_specs=(hbm, hbm, hbm),
        scratch_shapes=scratch,
        compiler_params=pltpu.CompilerParams(
            collective_id=0, has_side_effects=True, vmem_limit_bytes=60 * 2**20),
        name="transport_remap",
    )(in_lines(tracers), in_lines(courant_x), in_lines(courant_y), in_lines(thickness), level_weights)
    out, geo = pl.pallas_call(
        functools.partial(finish, rows, tiles),
        out_shape=(results, jax.ShapeDtypeStruct((lines, LANES), f32)),
        in_specs=[hbm] * 3 + [pl.BlockSpec(memory_space=pltpu.SMEM), hbm],
        out_specs=(hbm, hbm),
        scratch_shapes=[buffer(8, lines), buffer(chunks, sum_lines), buffer(span_lines), pltpu.VMEM((rows, nlon), f32),
                        buffer(span_lines), buffer(lines), dma((2, 8)), dma((4,))],
        compiler_params=pltpu.CompilerParams(vmem_limit_bytes=60 * 2**20),
        name="finish",
    )(result, above, spans, level_weights, surface_geo)
    return from_lines(out, levels, rows), from_lines(geo, levels, rows)


def solution(mesh):
    in_specs = (
        P(None, "lev", "lat", None),
        P("lev", "lat", None),
        P("lev", "lat", None),
        P("lev", "lat", None),
        P(),
        P("lat", None),
    )
    out_specs = (P(None, "lev", "lat", None), P("lev", "lat", None))
    run = functools.partial(body, mesh.shape["lat"] // 2)
    return jax.shard_map(run, mesh=mesh, in_specs=in_specs, out_specs=out_specs, check_vma=False)
```

```python
import functools

import jax
import jax.numpy as jnp
from jax import lax
from jax.experimental import pallas as pl
from jax.experimental.layout import Layout, with_layout_constraint
from jax.experimental.pallas import tpu as pltpu
from jax.sharding import PartitionSpec as P

SUBSTEPS = 4
HALO = 3
CHUNK = 4
LANES = 128
TOP_PRESSURE = 1.0
GAS_FACTOR = 0.3
SHIFTS = (-3, -2, 2, 3)


def face_weights(courant):
    size = jnp.abs(courant)
    rest = 1.0 - size
    scaled = courant * rest * (1.0 / 12.0)
    return scaled * rest, scaled * size, courant * size * (3.0 - 2.0 * size)


def stencil_weights(courant):
    p, q, r = face_weights(courant)
    pos = courant > 0.0
    qp, rp = jnp.where(pos, q, 0.0), jnp.where(pos, r, 0.0)
    qn, rn = q - qp, r - rp
    p7 = 7.0 * p
    return [
        qp,
        -p - 7.0 * qp,
        p7 - 7.0 * qp + qn + rp,
        p7 + qp - 7.0 * qn + rn,
        -p - 7.0 * qn,
        qn,
    ]


def kernel(nsuper, rows, tiles, tr, cx, cy, th, wts_hbm, out, above, span_out, wts, lsem, spans,
           recvf, recvx, recvy, thr, field, zon, cxt, cyt, wz, wy, cyrow, cytop, tht, col, tmp, outp, geop, turns,
           s1, r1, sth, rth, sh, rh, sc, rc, sx, rx, so, ro, sg, rg, sp, fw):
    lat, lev = lax.axis_index("lat"), lax.axis_index("lev")
    sb, l = lat // 2, lat % 2
    h, c = lev // 2, lev % 2
    y = 2 * h + l
    both = 2 * rows
    chunks = rows // CHUNK
    pitch = 2 * tiles
    lines = CHUNK * pitch
    has_low, has_up = sb > 0, sb < nsuper - 1

    weights_copy = pltpu.make_async_copy(wts_hbm, wts, lsem)
    weights_copy.start()

    barrier = pltpu.get_barrier_semaphore()
    for k in range(1, 8):
        pl.semaphore_signal(barrier, 1, device_id=(2 * sb + (l ^ (k // 4)), lev ^ (k % 4)))

    @pl.when(has_low)
    def _():
        pl.semaphore_signal(barrier, 1, device_id=(lat - 2, lev))

    @pl.when(has_up)
    def _():
        pl.semaphore_signal(barrier, 1, device_id=(lat + 2, lev))

    @pl.when(jnp.logical_not(has_low))
    def _():
        for t in range(SUBSTEPS):
            zon[t, :, 0:8 * HALO, :] = jnp.zeros((tiles, 8 * HALO, LANES), jnp.float32)

    @pl.when(jnp.logical_not(has_up))
    def _():
        for t in range(SUBSTEPS):
            zon[t, :, 8 * (HALO + both):, :] = jnp.zeros((tiles, 8 * HALO, LANES), jnp.float32)
        cytop[...] = jnp.zeros((tiles, 8, LANES), jnp.float32)

    source = lax.broadcasted_iota(jnp.int32, (2 * LANES, LANES), 0) % LANES
    target = lax.broadcasted_iota(jnp.int32, (2 * LANES, LANES), 1)
    for n, steps in enumerate(SHIFTS):
        turns[:, n * LANES:(n + 1) * LANES] = jnp.where(
            source == (target + (steps + LANES)) % LANES, 1.0, 0.0).astype(jnp.bfloat16)

    others = 7 + has_low.astype(jnp.int32) + has_up.astype(jnp.int32)
    pl.semaphore_wait(barrier, others)

    def copy_to(src, dst, ssem, rsem, device):
        return pltpu.make_async_remote_copy(src, dst, ssem, rsem, device_id=device)

    def start(own, src, dst, ssem, rsem, device):
        if own is None:
            copy_to(src, dst, ssem, rsem, device).start()
            return

        @pl.when(own)
        def _():
            pltpu.make_async_copy(src, dst, rsem).start()

        @pl.when(jnp.logical_not(own))
        def _():
            copy_to(src, dst, ssem, rsem, device).start()

    def sent(own, src, dst, ssem, rsem, device):
        if own is None:
            copy_to(src, dst, ssem, rsem, device).wait_send()
            return

        @pl.when(jnp.logical_not(own))
        def _():
            copy_to(src, dst, ssem, rsem, device).wait_send()

    def arrived(dst, rsem):
        pltpu.make_async_copy(dst, dst, rsem).wait()

    def place(band, j):
        if isinstance(band, int):
            return j * CHUNK if band == 0 else rows - (j + 1) * CHUNK
        return jnp.where(band == 0, j * CHUNK, rows - (j + 1) * CHUNK)

    def span_of(band, j):
        first = place(band, j) * pitch
        return pl.ds(first if isinstance(first, int) else pl.multiple_of(first, 8), lines)

    courant_moves, field_moves = [], []
    slot = 2 * l + c
    for j in range(chunks):
        here = span_of(l, j)
        courant_moves.append([])
        field_moves.append([])
        for k in (3, 2, 1, 0):
            hd, ld = h ^ (k // 2), l ^ (k % 2)
            own = None if k else (c == h)
            device = (2 * sb + ld, 2 * hd + h)
            field_moves[j].append((own, tr.at[pl.ds(2 * (2 * hd + ld), 2), here], recvf.at[slot, :, here],
                                   s1.at[0, j, k], r1.at[0, j, slot], device))
            if k != 2:
                for kind, ref, target in ((1, cx, recvx), (2, cy, recvy)):
                    courant_moves[j].append((own, ref.at[here], target.at[slot, here],
                                             s1.at[kind, j, k], r1.at[kind, j, slot], device))
    thick_moves = []
    for k in (3, 2, 1, 0):
        hd, ld = h ^ (k // 2), l ^ (k % 2)
        own = None if k else (c == l)
        thick_moves.append((own, th, thr.at[lev], sth.at[k], rth.at[lev], (2 * sb + ld, 2 * hd + l)))

    passed = 2 * (1 - l) + (h ^ c)

    def forward(kind, j):
        ref = (recvx if kind == 1 else recvy).at[passed, span_of(1 - l, j)]
        return copy_to(ref, ref, fw.at[kind - 1, j], r1.at[kind, j, passed], (2 * sb + 1 - l, 2 * (1 - c) + c))

    def pass_on(j):
        for kind in (1, 2):
            ref = (recvx if kind == 1 else recvy).at[passed, span_of(1 - l, j)]
            arrived(ref, r1.at[kind, j, passed])
            forward(kind, j).start()

    def start_all(*groups):
        for group in groups:
            for move in group:
                start(*move)

    start_all(courant_moves[0], field_moves[0], courant_moves[1])
    weights_copy.wait()

    col_id = lax.broadcasted_iota(jnp.int32, (8, LANES), 1)
    keep = jnp.where(has_low, 1.0, 0.0)

    def shifted(values, steps):
        return merged([pltpu.roll(v, (-steps) % LANES, 1) for v in values], steps)

    def merged(turned, steps):
        count = len(turned)
        if steps < 0:
            return [jnp.where(col_id < -steps, turned[m - 1], turned[m]) for m in range(count)]
        return [jnp.where(col_id >= LANES - steps, turned[(m + 1) % count], turned[m]) for m in range(count)]

    def unpack(j, source, target, twice):
        def do(i, _):
            for band in range(2):
                r0 = place(band, j)
                for pair in range(2):
                    for a in range(2):
                        for f in range(2):
                            line = pl.ds(r0 * pitch + 2 * i + a, CHUNK, stride=pitch)
                            ref = source.at[2 * band + pair] if twice else source.at[2 * band + pair, f]
                            target[i, pl.ds(8 * (band * rows + r0) + 4 * f + 2 * pair + a, CHUNK, stride=8), :] = ref[line, :]
            return 0
        lax.fori_loop(0, tiles, do, 0)

    def both_places(j):
        return [place(0, j), rows + place(1, j)]

    def at_row(row):
        return pl.ds(8 * row if isinstance(row, int) else pl.multiple_of(8 * row, 8), 8)

    def zonal_weights(j):
        def do(d, _):
            for first in both_places(j):
                at8 = at_row(first + d)
                cxs = [cxt[m, at8, :] for m in range(tiles)]
                for m, (cxr, cxe) in enumerate(zip(cxs, shifted(cxs, 1))):
                    west, east = stencil_weights(cxr), stencil_weights(cxe)
                    wz[0, m, at8, :] = west[0]
                    for n in range(1, 6):
                        w = west[n] - east[n - 1]
                        wz[n, m, at8, :] = w + 1.0 if n == 3 else w
                    wz[6, m, at8, :] = -east[5]
            return 0
        lax.fori_loop(0, CHUNK, do, 0)

    def meridional_weights(j):
        def do(i, _):
            for first in both_places(j):
                for d in range(CHUNK):
                    at8 = at_row(first + d)
                    cyr = cyt[i, at8, :]
                    if first + d == 0:
                        cyr = keep * cyr
                        cyrow[i] = cyr
                    for n, w in enumerate(face_weights(cyr)):
                        wy[n, i, at8, :] = w
            return 0
        lax.fori_loop(0, tiles, do, 0)

    def low_row():
        return copy_to(cyrow, cytop, sc, rc, (lat - 2, lev))

    def zonal(t, rows_here):
        f = [[field[t, m, at_row(row), :] for m in range(tiles)] for row in rows_here]
        flat = jnp.concatenate([v for one in f for v in one], axis=0)
        head = flat.astype(jnp.bfloat16)
        rest = (flat - head.astype(jnp.float32)).astype(jnp.bfloat16)
        parts = jnp.concatenate([head, rest], axis=1)
        turned = {}
        for n in range(0, len(SHIFTS), 2):
            moved = jnp.dot(parts, turns[:, n * LANES:(n + 2) * LANES], preferred_element_type=jnp.float32)
            turned[SHIFTS[n]], turned[SHIFTS[n + 1]] = moved[:, :LANES], moved[:, LANES:]
        for n, row in enumerate(rows_here):
            at8 = at_row(row)
            total = [wz[3, m, at8, :] * f[n][m] for m in range(tiles)]
            for k in (0, 1, 2, 4, 5, 6):
                steps = k - 3
                if steps in turned:
                    first = 8 * tiles * n
                    moved = merged([turned[steps][first + 8 * m:first + 8 * m + 8] for m in range(tiles)], steps)
                else:
                    moved = shifted(f[n], steps)
                total = [total[m] + wz[k, m, at8, :] * moved[m] for m in range(tiles)]
            to8 = at_row(row + HALO)
            for m in range(tiles):
                zon[t, m, to8, :] = total[m]

    def meridional(t, starts, n):
        def do(i, _):
            for r0 in starts:
                def z(row):
                    return zon[t, i, 8 * (row + HALO):8 * (row + HALO) + 8, :]

                window = [z(r0 + d) for d in range(-3, 3)]
                sums = [window[m] + window[m + 1] for m in range(5)]

                def face(m):
                    return 8.0 * sums[m] - (sums[m - 1] + sums[m + 1])
                values = [face(1), face(2), face(3)]
                before = None
                for row in range(r0, r0 + n + 1):
                    at8 = at_row(row)
                    p, q, r = wy[0, i, at8, :], wy[1, i, at8, :], wy[2, i, at8, :]
                    pos = p > 0.0
                    flux = p * values[1] - q * jnp.where(pos, values[0], values[2]) + r * jnp.where(
                        pos, window[2], window[3])
                    if before is not None:
                        field[t + 1, i, at_row(row - 1), :] = window[2] - (flux - before)
                    before = flux
                    if row < r0 + n:
                        window = window[1:] + [z(row + 3)]
                        sums = sums[1:] + [window[4] + window[5]]
                        values = values[1:] + [face(3)]
            return 0
        lax.fori_loop(0, tiles, do, 0, unroll=True)

    edge = 8 * HALO
    top = 8 * both
    ends = [0, both - HALO]

    def to_low(t):
        return copy_to(zon.at[t, :, pl.ds(edge, edge)], zon.at[t, :, pl.ds(edge + top, edge)],
                       sh.at[t, 0], rh.at[t, 0], (lat - 2, lev))

    def to_up(t):
        return copy_to(zon.at[t, :, pl.ds(top, edge)], zon.at[t, :, pl.ds(0, edge)],
                       sh.at[t, 1], rh.at[t, 1], (lat + 2, lev))

    def send_halo(t):
        zonal(t, [first + d for first in ends for d in range(HALO)])

        @pl.when(has_low)
        def _():
            to_low(t).start()

        @pl.when(has_up)
        def _():
            to_up(t).start()

    def wait_halo(t):
        @pl.when(has_low)
        def _():
            to_up(t).wait_recv()

        @pl.when(has_up)
        def _():
            to_low(t).wait_recv()

    def take_fields(j):
        for s in range(4):
            arrived(recvf.at[s, :, span_of(s // 2, j)], r1.at[0, j, s])
        unpack(j, recvf, field.at[0], False)

    def take_courant(j):
        for kind, ref, target in ((1, recvx, cxt), (2, recvy, cyt)):
            for s in range(4):
                @pl.when(s != passed)
                def _():
                    arrived(ref.at[s, span_of(s // 2, j)], r1.at[kind, j, s])
            unpack(j, ref, target, True)
        zonal_weights(j)
        meridional_weights(j)

    part = 8 * CHUNK

    def swap(j):
        theirs = pl.multiple_of(8 * ((1 - c) * rows + place(1 - c, j)), part)
        return copy_to(field.at[SUBSTEPS, :, pl.ds(theirs, part)], col.at[c, j], sx.at[j], rx.at[j], (lat, lev ^ 1))

    def send_swap(j):
        swap(j).start()
        ours = pl.multiple_of(8 * (c * rows + place(c, j)), part)
        col[c, j] = field[SUBSTEPS, :, pl.ds(ours, part), :]

    full = (8, LANES)

    def take_thickness():
        for s in range(4):
            arrived(thr.at[s], rth.at[s])

        def do(i, _):
            for j in range(chunks):
                first = place(c, j) * pitch + 2 * i
                for k in range(8):
                    piece = thr[k // 2, pl.ds(first + k % 2, CHUNK, stride=pitch), :]
                    for f in range(2):
                        tht[j, i, pl.ds(8 * k + f, CHUNK, stride=2), :] = piece
            for r0, n in ((0, 8), (8, rows - 8)):
                total = None
                for k in range(8):
                    piece = thr[k // 2, pl.ds(r0 * pitch + 2 * i + k % 2, n, stride=pitch), :]
                    total = piece if total is None else total + piece
                spans[pl.ds(r0 * tiles + i, n, stride=tiles), :] = total
            return 0
        lax.fori_loop(0, tiles, do, 0)

        @pl.when(c == l)
        def _():
            keep_spans.start()
            give_spans.start()

    keep_spans = pltpu.make_async_copy(spans, span_out, sp.at[0])
    give_spans = copy_to(spans, span_out, sp.at[1], sp.at[2], (lat, lev ^ 1))

    def columns(j, i):
        weights = [jnp.full(full, wts[k], jnp.float32) for k in range(8)]
        whole = weights[0]
        for k in range(1, 8):
            whole = whole + weights[k]
        inverse = 1.0 / whole
        thick = [tht[j, i, 8 * k:8 * k + 8, :] for k in range(8)]
        bounds = [jnp.full(full, TOP_PRESSURE, jnp.float32)]
        for k in range(8):
            bounds.append(bounds[-1] + thick[k])
        span = bounds[8] - TOP_PRESSURE
        low, up, total = [], [], None
        for k in range(8):
            total = weights[k] if total is None else total + weights[k]
            low.append(TOP_PRESSURE + span * (total * inverse))
            up.append(low[k] - span * (weights[k] * inverse))
        return thick, bounds, low, up

    def remap(j):
        def do(i, _):
            thick, bounds, low, up = columns(j, i)
            density = [col[k // 4, j, i, pl.ds(k % 4, 8, stride=4), :] / thick[k] for k in range(8)]
            for k in range(8):
                total = None
                for n in range(8):
                    cut = jnp.maximum(0.0, jnp.minimum(bounds[n + 1], low[k]) - jnp.maximum(bounds[n], up[k]))
                    total = density[n] * cut if total is None else total + density[n] * cut
                tmp[j, i, 8 * k:8 * k + 8, :] = total
            for k in range(8):
                for f in range(2):
                    outp[k // 2, j, f, pl.ds(2 * i + k % 2, CHUNK, stride=pitch), :] = (
                        tmp[j, i, pl.ds(8 * k + f, CHUNK, stride=2), :])
            return 0
        lax.fori_loop(0, tiles, do, 0)

    def integrate(j):
        def do(i, _):
            _, _, low, up = columns(j, i)
            total = None
            for k in range(7, -1, -1):
                layer = GAS_FACTOR * tmp[j, i, 8 * k:8 * k + 8, :] / (low[k] - up[k]) * jnp.log(low[k] / up[k])
                total = layer if total is None else total + layer
                tmp[j, i, 8 * k:8 * k + 8, :] = total
            for n in range(3):
                geop[n, j, pl.ds(i, CHUNK, stride=tiles), :] = tmp[j, i, pl.ds(8 * (2 * n + 2), CHUNK, stride=2), :]
            return 0
        lax.fori_loop(0, tiles, do, 0)

    def result_moves(j):
        here = span_of(c, j)
        for k in (3, 2, 1, 0):
            gd = lev ^ k
            yield (None if k else (c == l), outp.at[gd, j], out.at[pl.ds(2 * y, 2), here],
                   so.at[j, k], ro.at[j, y], (2 * sb + c, gd))

    def integral_moves(j):
        for n in range(3):
            yield (None if n else (c == 0), geop.at[n, j], above.at[j], sg.at[j, n], rg.at[j], (2 * sb + c, n))

    def send_results(j):
        swap(j).wait_recv()
        remap(j)
        for move in result_moves(j):
            start(*move)

    def send_integrals(*which):
        @pl.when(y == 0)
        def _():
            for j in which:
                integrate(j)
                for move in integral_moves(j):
                    start(*move)

    pass_on(0)
    start_all(courant_moves[2], field_moves[1])
    take_courant(0)

    @pl.when(has_low)
    def _():
        low_row().start()
    take_fields(0)
    send_halo(0)
    pass_on(1)
    zonal(0, [HALO, both - HALO - 1])
    pass_on(2)
    start_all(field_moves[2], thick_moves)

    take_courant(1)
    take_fields(1)
    zonal(0, [first + d for first in both_places(1) for d in range(CHUNK)])

    @pl.when(has_up)
    def _():
        low_row().wait_recv()
    for n, w in enumerate(face_weights(cytop[...])):
        wy[n, :, top:top + 8, :] = w
    wait_halo(0)
    meridional(0, [0, both - 5], 5)
    send_halo(1)
    zonal(1, [3, 4, both - 5, both - 4])

    take_courant(2)
    take_fields(2)
    zonal(0, list(range(8, 16)))
    meridional(0, [5], both - 10)
    zonal(1, list(range(5, 19)))
    wait_halo(1)
    meridional(1, ends, HALO)
    send_halo(2)
    meridional(1, [HALO], both - 2 * HALO)
    zonal(2, list(range(3, 13)))
    zonal(2, list(range(13, 21)))
    meridional(2, [5], both - 10)
    zonal(3, list(range(5, 19)))
    meridional(3, [8], 8)
    send_swap(2)

    take_thickness()
    send_results(2)

    wait_halo(2)
    meridional(2, ends, HALO)
    send_halo(3)
    meridional(2, [HALO, both - 5], 2)
    zonal(3, [3, 4, both - 5, both - 4])
    meridional(3, [HALO, both - 8], 5)
    send_swap(1)
    send_integrals(2)
    send_results(1)

    wait_halo(3)
    meridional(3, ends, HALO)
    send_swap(0)
    send_integrals(1)
    send_results(0)
    send_integrals(0)

    @pl.when(lev < 3)
    def _():
        for j in range(chunks):
            arrived(above.at[j], rg.at[j])

    @pl.when(c == l)
    def _():
        keep_spans.wait()
        give_spans.wait_send()

    @pl.when(c != l)
    def _():
        give_spans.wait_recv()
    for j in range(chunks):
        for s in range(4):
            arrived(out.at[pl.ds(2 * s, 2), span_of(l, j)], ro.at[j, s])

    for group in courant_moves + field_moves + [thick_moves]:
        for move in group:
            sent(*move)
    for j in range(chunks):
        for kind in (1, 2):
            forward(kind, j).wait_send()
    for j in range(chunks):
        swap(j).wait_send()
        for move in result_moves(j):
            sent(*move)

    @pl.when(y == 0)
    def _():
        for j in range(chunks):
            for move in integral_moves(j):
                sent(*move)

    @pl.when(has_low)
    def _():
        low_row().wait_send()
        for t in range(SUBSTEPS):
            to_low(t).wait_send()

    @pl.when(has_up)
    def _():
        for t in range(SUBSTEPS):
            to_up(t).wait_send()


def finish(rows, tiles, result, above, span_in, wts, surface, out, geo, held, over, spans, sgeo, sums, total, sems, gsems):
    lat, lev = lax.axis_index("lat"), lax.axis_index("lev")
    l = lat % 2
    pitch = 2 * tiles
    loads = [pltpu.make_async_copy(above, over, gsems.at[0]), pltpu.make_async_copy(span_in, spans, gsems.at[1]),
             pltpu.make_async_copy(surface, sgeo, gsems.at[2])]
    takes = [pltpu.make_async_copy(result.at[f], held.at[f], sems.at[0, f]) for f in range(8)]
    gives = [pltpu.make_async_copy(held.at[f], out.at[f], sems.at[1, f]) for f in range(8)]
    for copy in takes[:1] + loads + takes[1:]:
        copy.start()
    for copy in loads:
        copy.wait()
    takes[0].wait()
    gives[0].start()
    for j in range(rows // CHUNK):
        row = jnp.where(l == 0, j * CHUNK, rows - (j + 1) * CHUNK)
        for i in range(tiles):
            sums[pl.ds(row * tiles + i, CHUNK, stride=tiles), :] = over[j, pl.ds(i, CHUNK, stride=tiles), :]
    for r0, n in ((0, 8), (8, rows - 8)):
        shape = (n, LANES)
        whole, below, mine = None, jnp.zeros(shape, jnp.float32), [None, None]
        for k in range(8):
            weight = jnp.full(shape, wts[k], jnp.float32)
            whole = weight if whole is None else whole + weight
            below = below + jnp.where(k < 2 * lev, weight, 0.0)
            mine[k % 2] = weight if k < 2 else jnp.where(k // 2 == lev, weight, mine[k % 2])
        inverse = 1.0 / whole
        shares = [mine[0] * inverse, mine[1] * inverse]
        fractions = [(below + mine[0]) * inverse, (below + mine[0] + mine[1]) * inverse]
        for i in range(tiles):
            span = spans[pl.ds(r0 * tiles + i, n, stride=tiles), :]
            value = jnp.where(lev < 3, sums[pl.ds(r0 * tiles + i, n, stride=tiles), :], 0.0)
            value = value + sgeo[r0:r0 + n, i * LANES:(i + 1) * LANES]
            for a in (1, 0):
                here = pl.ds(r0 * pitch + 2 * i + a, n, stride=pitch)
                low = TOP_PRESSURE + span * fractions[a]
                up = low - span * shares[a]
                value = value + GAS_FACTOR * held[0, here, :] / (low - up) * jnp.log(low / up)
                total[here, :] = value
    store = pltpu.make_async_copy(total, geo, gsems.at[3])
    store.start()
    for take, give in zip(takes[1:], gives[1:]):
        take.wait()
        give.start()
    for copy in gives + [store]:
        copy.wait()


def in_lines(array):
    lead = array.ndim - 3
    levels, rows, nlon = array.shape[lead:]
    tiles = nlon // LANES
    split = array.reshape(array.shape[:-1] + (tiles, LANES))
    order = tuple(range(lead)) + (lead + 1, lead + 2, lead, lead + 3)
    split = with_layout_constraint(split, Layout(major_to_minor=order))
    return jnp.transpose(split, order).reshape(array.shape[:lead] + (rows * tiles * levels, LANES))


def from_lines(array, levels, rows):
    lead = array.ndim - 2
    tiles = array.shape[-2] // (levels * rows)
    split = array.reshape(array.shape[:lead] + (rows, tiles, levels, LANES))
    split = jnp.transpose(split, tuple(range(lead)) + (lead + 2, lead, lead + 1, lead + 3))
    order = tuple(range(lead)) + (lead + 1, lead + 2, lead, lead + 3)
    split = with_layout_constraint(split, Layout(major_to_minor=order))
    return split.reshape(array.shape[:lead] + (levels, rows, tiles * LANES))


def body(nsuper, tracers, courant_x, courant_y, thickness, level_weights, surface_geo):
    levels, rows, nlon = thickness.shape
    tiles = nlon // LANES
    f32 = jnp.float32
    hbm = pl.BlockSpec(memory_space=pltpu.HBM)
    both = 2 * rows
    lines = rows * tiles * levels
    chunks = rows // CHUNK
    sum_lines = -(-CHUNK * tiles // 8) * 8
    span_lines = -(-rows * tiles // 8) * 8

    def buffer(*shape):
        return pltpu.VMEM(shape + (LANES,), f32)

    dma = pltpu.SemaphoreType.DMA
    scratch = [
        pltpu.SMEM((8,), f32), dma, buffer(span_lines),
        buffer(4, 2, lines), buffer(4, lines), buffer(4, lines), buffer(4, lines),
        buffer(SUBSTEPS + 1, tiles, 8 * both), buffer(SUBSTEPS, tiles, 8 * (both + 2 * HALO)),
        buffer(tiles, 8 * both), buffer(tiles, 8 * both),
        buffer(7, tiles, 8 * both), buffer(3, tiles, 8 * (both + 1)),
        buffer(tiles, 8), buffer(tiles, 8), buffer(chunks, tiles, 64),
        buffer(2, chunks, tiles, 8 * CHUNK), buffer(chunks, tiles, 64),
        buffer(4, chunks, 2, lines // chunks), buffer(3, chunks, sum_lines),
        pltpu.VMEM((2 * LANES, len(SHIFTS) * LANES), jnp.bfloat16),
        dma((3, chunks, 4)), dma((3, chunks, 4)), dma((4,)), dma((4,)), dma((SUBSTEPS, 2)), dma((SUBSTEPS, 2)),
        dma, dma, dma((chunks,)), dma((chunks,)),
        dma((chunks, 4)), dma((chunks, 4)), dma((chunks, 3)), dma((chunks,)), dma((3,)), dma((2, chunks)),
    ]
    results = jax.ShapeDtypeStruct((8, lines, LANES), f32)
    result, above, spans = pl.pallas_call(
        functools.partial(kernel, nsuper, rows, tiles),
        out_shape=(results, jax.ShapeDtypeStruct((chunks, sum_lines, LANES), f32),
                   jax.ShapeDtypeStruct((span_lines, LANES), f32)),
        in_specs=[hbm] * 5,
        out_specs=(hbm, hbm, hbm),
        scratch_shapes=scratch,
        compiler_params=pltpu.CompilerParams(
            collective_id=0, has_side_effects=True, vmem_limit_bytes=60 * 2**20),
        name="transport_remap",
    )(in_lines(tracers), in_lines(courant_x), in_lines(courant_y), in_lines(thickness), level_weights)
    out, geo = pl.pallas_call(
        functools.partial(finish, rows, tiles),
        out_shape=(results, jax.ShapeDtypeStruct((lines, LANES), f32)),
        in_specs=[hbm] * 3 + [pl.BlockSpec(memory_space=pltpu.SMEM), hbm],
        out_specs=(hbm, hbm),
        scratch_shapes=[buffer(8, lines), buffer(chunks, sum_lines), buffer(span_lines), pltpu.VMEM((rows, nlon), f32),
                        buffer(span_lines), buffer(lines), dma((2, 8)), dma((4,))],
        compiler_params=pltpu.CompilerParams(vmem_limit_bytes=60 * 2**20),
        name="finish",
    )(result, above, spans, level_weights, surface_geo)
    return from_lines(out, levels, rows), from_lines(geo, levels, rows)


def solution(mesh):
    in_specs = (
        P(None, "lev", "lat", None),
        P("lev", "lat", None),
        P("lev", "lat", None),
        P("lev", "lat", None),
        P(),
        P("lat", None),
    )
    out_specs = (P(None, "lev", "lat", None), P("lev", "lat", None))
    run = functools.partial(body, mesh.shape["lat"] // 2)
    return jax.shard_map(run, mesh=mesh, in_specs=in_specs, out_specs=out_specs, check_vma=False)
```

```python
import functools

import jax
import jax.numpy as jnp
from jax import lax
from jax.experimental import pallas as pl
from jax.experimental.layout import Layout, with_layout_constraint
from jax.experimental.pallas import tpu as pltpu
from jax.sharding import PartitionSpec as P

SUBSTEPS = 4
HALO = 3
CHUNK = 4
LANES = 128
TOP_PRESSURE = 1.0
GAS_FACTOR = 0.3
SHIFTS = (-3, -2, 2, 3)


def face_weights(courant):
    size = jnp.abs(courant)
    rest = 1.0 - size
    scaled = courant * rest * (1.0 / 12.0)
    return scaled * rest, scaled * size, courant * size * (3.0 - 2.0 * size)


def stencil_weights(courant):
    p, q, r = face_weights(courant)
    pos = courant > 0.0
    qp, rp = jnp.where(pos, q, 0.0), jnp.where(pos, r, 0.0)
    qn, rn = q - qp, r - rp
    p7 = 7.0 * p
    return [
        qp,
        -p - 7.0 * qp,
        p7 - 7.0 * qp + qn + rp,
        p7 + qp - 7.0 * qn + rn,
        -p - 7.0 * qn,
        qn,
    ]


def kernel(nsuper, rows, tiles, tr, cx, cy, th, wts_hbm, out, above, span_out, wts, lsem, spans,
           recvf, recvx, recvy, thr, field, zon, cxt, cyt, wz, wy, cyrow, cytop, tht, col, tmp, outp, geop, turns,
           s1, r1, sth, rth, sh, rh, sc, rc, sx, rx, so, ro, sg, rg, sp, fw):
    lat, lev = lax.axis_index("lat"), lax.axis_index("lev")
    sb, l = lat // 2, lat % 2
    h, c = lev // 2, lev % 2
    y = 2 * h + l
    both = 2 * rows
    chunks = rows // CHUNK
    pitch = 2 * tiles
    lines = CHUNK * pitch
    has_low, has_up = sb > 0, sb < nsuper - 1

    weights_copy = pltpu.make_async_copy(wts_hbm, wts, lsem)
    weights_copy.start()

    barrier = pltpu.get_barrier_semaphore()
    for k in range(1, 8):
        pl.semaphore_signal(barrier, 1, device_id=(2 * sb + (l ^ (k // 4)), lev ^ (k % 4)))

    @pl.when(has_low)
    def _():
        pl.semaphore_signal(barrier, 1, device_id=(lat - 2, lev))

    @pl.when(has_up)
    def _():
        pl.semaphore_signal(barrier, 1, device_id=(lat + 2, lev))

    @pl.when(jnp.logical_not(has_low))
    def _():
        for t in range(SUBSTEPS):
            zon[t, :, 0:8 * HALO, :] = jnp.zeros((tiles, 8 * HALO, LANES), jnp.float32)

    @pl.when(jnp.logical_not(has_up))
    def _():
        for t in range(SUBSTEPS):
            zon[t, :, 8 * (HALO + both):, :] = jnp.zeros((tiles, 8 * HALO, LANES), jnp.float32)
        cytop[...] = jnp.zeros((tiles, 8, LANES), jnp.float32)

    source = lax.broadcasted_iota(jnp.int32, (2 * LANES, LANES), 0) % LANES
    target = lax.broadcasted_iota(jnp.int32, (2 * LANES, LANES), 1)
    for n, steps in enumerate(SHIFTS):
        turns[:, n * LANES:(n + 1) * LANES] = jnp.where(
            source == (target + (steps + LANES)) % LANES, 1.0, 0.0).astype(jnp.bfloat16)

    others = 7 + has_low.astype(jnp.int32) + has_up.astype(jnp.int32)
    pl.semaphore_wait(barrier, others)

    def copy_to(src, dst, ssem, rsem, device):
        return pltpu.make_async_remote_copy(src, dst, ssem, rsem, device_id=device)

    def start(own, src, dst, ssem, rsem, device):
        if own is None:
            copy_to(src, dst, ssem, rsem, device).start()
            return

        @pl.when(own)
        def _():
            pltpu.make_async_copy(src, dst, rsem).start()

        @pl.when(jnp.logical_not(own))
        def _():
            copy_to(src, dst, ssem, rsem, device).start()

    def sent(own, src, dst, ssem, rsem, device):
        if own is None:
            copy_to(src, dst, ssem, rsem, device).wait_send()
            return

        @pl.when(jnp.logical_not(own))
        def _():
            copy_to(src, dst, ssem, rsem, device).wait_send()

    def arrived(dst, rsem):
        pltpu.make_async_copy(dst, dst, rsem).wait()

    def place(band, j):
        if isinstance(band, int):
            return j * CHUNK if band == 0 else rows - (j + 1) * CHUNK
        return jnp.where(band == 0, j * CHUNK, rows - (j + 1) * CHUNK)

    def span_of(band, j):
        first = place(band, j) * pitch
        return pl.ds(first if isinstance(first, int) else pl.multiple_of(first, 8), lines)

    courant_moves, field_moves = [], []
    slot = 2 * l + c
    for j in range(chunks):
        here = span_of(l, j)
        courant_moves.append([])
        field_moves.append([])
        for k in (3, 2, 1, 0):
            hd, ld = h ^ (k // 2), l ^ (k % 2)
            own = None if k else (c == h)
            device = (2 * sb + ld, 2 * hd + h)
            field_moves[j].append((own, tr.at[pl.ds(2 * (2 * hd + ld), 2), here], recvf.at[slot, :, here],
                                   s1.at[0, j, k], r1.at[0, j, slot], device))
            if k != 2:
                for kind, ref, target in ((1, cx, recvx), (2, cy, recvy)):
                    courant_moves[j].append((own, ref.at[here], target.at[slot, here],
                                             s1.at[kind, j, k], r1.at[kind, j, slot], device))
    thick_moves = []
    for k in (3, 2, 1, 0):
        hd, ld = h ^ (k // 2), l ^ (k % 2)
        own = None if k else (c == l)
        thick_moves.append((own, th, thr.at[lev], sth.at[k], rth.at[lev], (2 * sb + ld, 2 * hd + l)))

    passed = 2 * (1 - l) + (h ^ c)

    def forward(kind, j):
        ref = (recvx if kind == 1 else recvy).at[passed, span_of(1 - l, j)]
        return copy_to(ref, ref, fw.at[kind - 1, j], r1.at[kind, j, passed], (2 * sb + 1 - l, 2 * (1 - c) + c))

    def pass_on(j):
        for kind in (1, 2):
            ref = (recvx if kind == 1 else recvy).at[passed, span_of(1 - l, j)]
            arrived(ref, r1.at[kind, j, passed])
            forward(kind, j).start()

    def start_all(*groups):
        for group in groups:
            for move in group:
                start(*move)

    start_all(courant_moves[0], field_moves[0], courant_moves[1])
    weights_copy.wait()

    col_id = lax.broadcasted_iota(jnp.int32, (8, LANES), 1)
    keep = jnp.where(has_low, 1.0, 0.0)

    def shifted(values, steps):
        return merged([pltpu.roll(v, (-steps) % LANES, 1) for v in values], steps)

    def merged(turned, steps):
        count = len(turned)
        if steps < 0:
            return [jnp.where(col_id < -steps, turned[m - 1], turned[m]) for m in range(count)]
        return [jnp.where(col_id >= LANES - steps, turned[(m + 1) % count], turned[m]) for m in range(count)]

    def unpack(j, source, target, twice):
        def do(i, _):
            for band in range(2):
                r0 = place(band, j)
                for pair in range(2):
                    for a in range(2):
                        for f in range(2):
                            line = pl.ds(r0 * pitch + 2 * i + a, CHUNK, stride=pitch)
                            ref = source.at[2 * band + pair] if twice else source.at[2 * band + pair, f]
                            target[i, pl.ds(8 * (band * rows + r0) + 4 * f + 2 * pair + a, CHUNK, stride=8), :] = ref[line, :]
            return 0
        lax.fori_loop(0, tiles, do, 0)

    def both_places(j):
        return [place(0, j), rows + place(1, j)]

    def at_row(row):
        return pl.ds(8 * row if isinstance(row, int) else pl.multiple_of(8 * row, 8), 8)

    def zonal_weights(j):
        def do(d, _):
            for first in both_places(j):
                at8 = at_row(first + d)
                cxs = [cxt[m, at8, :] for m in range(tiles)]
                for m, (cxr, cxe) in enumerate(zip(cxs, shifted(cxs, 1))):
                    west, east = stencil_weights(cxr), stencil_weights(cxe)
                    wz[0, m, at8, :] = west[0]
                    for n in range(1, 6):
                        w = west[n] - east[n - 1]
                        wz[n, m, at8, :] = w + 1.0 if n == 3 else w
                    wz[6, m, at8, :] = -east[5]
            return 0
        lax.fori_loop(0, CHUNK, do, 0)

    def meridional_weights(j):
        def do(i, _):
            for first in both_places(j):
                for d in range(CHUNK):
                    at8 = at_row(first + d)
                    cyr = cyt[i, at8, :]
                    if first + d == 0:
                        cyr = keep * cyr
                        cyrow[i] = cyr
                    for n, w in enumerate(face_weights(cyr)):
                        wy[n, i, at8, :] = w
            return 0
        lax.fori_loop(0, tiles, do, 0)

    def low_row():
        return copy_to(cyrow, cytop, sc, rc, (lat - 2, lev))

    def zonal(t, rows_here):
        f = [[field[t, m, at_row(row), :] for m in range(tiles)] for row in rows_here]
        flat = jnp.concatenate([v for one in f for v in one], axis=0)
        head = flat.astype(jnp.bfloat16)
        rest = (flat - head.astype(jnp.float32)).astype(jnp.bfloat16)
        parts = jnp.concatenate([head, rest], axis=1)
        turned = {}
        for n in range(0, len(SHIFTS), 2):
            moved = jnp.dot(parts, turns[:, n * LANES:(n + 2) * LANES], preferred_element_type=jnp.float32)
            turned[SHIFTS[n]], turned[SHIFTS[n + 1]] = moved[:, :LANES], moved[:, LANES:]
        for n, row in enumerate(rows_here):
            at8 = at_row(row)
            total = [wz[3, m, at8, :] * f[n][m] for m in range(tiles)]
            for k in (0, 1, 2, 4, 5, 6):
                steps = k - 3
                if steps in turned:
                    first = 8 * tiles * n
                    moved = merged([turned[steps][first + 8 * m:first + 8 * m + 8] for m in range(tiles)], steps)
                else:
                    moved = shifted(f[n], steps)
                total = [total[m] + wz[k, m, at8, :] * moved[m] for m in range(tiles)]
            to8 = at_row(row + HALO)
            for m in range(tiles):
                zon[t, m, to8, :] = total[m]

    def meridional(t, starts, n):
        def do(i, _):
            for r0 in starts:
                def z(row):
                    return zon[t, i, 8 * (row + HALO):8 * (row + HALO) + 8, :]

                window = [z(r0 + d) for d in range(-3, 3)]
                sums = [window[m] + window[m + 1] for m in range(5)]

                def face(m):
                    return 8.0 * sums[m] - (sums[m - 1] + sums[m + 1])
                values = [face(1), face(2), face(3)]
                before = None
                for row in range(r0, r0 + n + 1):
                    at8 = at_row(row)
                    p, q, r = wy[0, i, at8, :], wy[1, i, at8, :], wy[2, i, at8, :]
                    pos = p > 0.0
                    flux = p * values[1] - q * jnp.where(pos, values[0], values[2]) + r * jnp.where(
                        pos, window[2], window[3])
                    if before is not None:
                        field[t + 1, i, at_row(row - 1), :] = window[2] - (flux - before)
                    before = flux
                    if row < r0 + n:
                        window = window[1:] + [z(row + 3)]
                        sums = sums[1:] + [window[4] + window[5]]
                        values = values[1:] + [face(3)]
            return 0
        lax.fori_loop(0, tiles, do, 0, unroll=True)

    edge = 8 * HALO
    top = 8 * both
    ends = [0, both - HALO]

    def to_low(t):
        return copy_to(zon.at[t, :, pl.ds(edge, edge)], zon.at[t, :, pl.ds(edge + top, edge)],
                       sh.at[t, 0], rh.at[t, 0], (lat - 2, lev))

    def to_up(t):
        return copy_to(zon.at[t, :, pl.ds(top, edge)], zon.at[t, :, pl.ds(0, edge)],
                       sh.at[t, 1], rh.at[t, 1], (lat + 2, lev))

    def send_halo(t):
        zonal(t, [first + d for first in ends for d in range(HALO)])

        @pl.when(has_low)
        def _():
            to_low(t).start()

        @pl.when(has_up)
        def _():
            to_up(t).start()

    def wait_halo(t):
        @pl.when(has_low)
        def _():
            to_up(t).wait_recv()

        @pl.when(has_up)
        def _():
            to_low(t).wait_recv()

    def take_fields(j):
        for s in range(4):
            arrived(recvf.at[s, :, span_of(s // 2, j)], r1.at[0, j, s])
        unpack(j, recvf, field.at[0], False)

    def take_courant(j):
        for kind, ref, target in ((1, recvx, cxt), (2, recvy, cyt)):
            for s in range(4):
                @pl.when(s != passed)
                def _():
                    arrived(ref.at[s, span_of(s // 2, j)], r1.at[kind, j, s])
            unpack(j, ref, target, True)
        zonal_weights(j)
        meridional_weights(j)

    part = 8 * CHUNK

    def swap(j):
        theirs = pl.multiple_of(8 * ((1 - c) * rows + place(1 - c, j)), part)
        return copy_to(field.at[SUBSTEPS, :, pl.ds(theirs, part)], col.at[c, j], sx.at[j], rx.at[j], (lat, lev ^ 1))

    def send_swap(j):
        swap(j).start()
        ours = pl.multiple_of(8 * (c * rows + place(c, j)), part)
        col[c, j] = field[SUBSTEPS, :, pl.ds(ours, part), :]

    full = (8, LANES)

    def take_thickness():
        for s in range(4):
            arrived(thr.at[s], rth.at[s])

        def do(i, _):
            for j in range(chunks):
                first = place(c, j) * pitch + 2 * i
                for k in range(8):
                    piece = thr[k // 2, pl.ds(first + k % 2, CHUNK, stride=pitch), :]
                    for f in range(2):
                        tht[j, i, pl.ds(8 * k + f, CHUNK, stride=2), :] = piece
            for r0, n in ((0, 8), (8, rows - 8)):
                total = None
                for k in range(8):
                    piece = thr[k // 2, pl.ds(r0 * pitch + 2 * i + k % 2, n, stride=pitch), :]
                    total = piece if total is None else total + piece
                spans[pl.ds(r0 * tiles + i, n, stride=tiles), :] = total
            return 0
        lax.fori_loop(0, tiles, do, 0)

        @pl.when(c == l)
        def _():
            keep_spans.start()
            give_spans.start()

    keep_spans = pltpu.make_async_copy(spans, span_out, sp.at[0])
    give_spans = copy_to(spans, span_out, sp.at[1], sp.at[2], (lat, lev ^ 1))

    def columns(j, i):
        weights = [jnp.full(full, wts[k], jnp.float32) for k in range(8)]
        whole = weights[0]
        for k in range(1, 8):
            whole = whole + weights[k]
        inverse = 1.0 / whole
        thick = [tht[j, i, 8 * k:8 * k + 8, :] for k in range(8)]
        bounds = [jnp.full(full, TOP_PRESSURE, jnp.float32)]
        for k in range(8):
            bounds.append(bounds[-1] + thick[k])
        span = bounds[8] - TOP_PRESSURE
        low, up, total = [], [], None
        for k in range(8):
            total = weights[k] if total is None else total + weights[k]
            low.append(TOP_PRESSURE + span * (total * inverse))
            up.append(low[k] - span * (weights[k] * inverse))
        return thick, bounds, low, up

    def remap(j):
        def do(i, _):
            thick, bounds, low, up = columns(j, i)
            density = [col[k // 4, j, i, pl.ds(k % 4, 8, stride=4), :] / thick[k] for k in range(8)]
            for k in range(8):
                total = None
                for n in range(8):
                    cut = jnp.maximum(0.0, jnp.minimum(bounds[n + 1], low[k]) - jnp.maximum(bounds[n], up[k]))
                    total = density[n] * cut if total is None else total + density[n] * cut
                tmp[j, i, 8 * k:8 * k + 8, :] = total
            for k in range(8):
                for f in range(2):
                    outp[k // 2, j, f, pl.ds(2 * i + k % 2, CHUNK, stride=pitch), :] = (
                        tmp[j, i, pl.ds(8 * k + f, CHUNK, stride=2), :])
            return 0
        lax.fori_loop(0, tiles, do, 0)

    def integrate(j):
        def do(i, _):
            _, _, low, up = columns(j, i)
            total = None
            for k in range(7, -1, -1):
                layer = GAS_FACTOR * tmp[j, i, 8 * k:8 * k + 8, :] / (low[k] - up[k]) * jnp.log(low[k] / up[k])
                total = layer if total is None else total + layer
                tmp[j, i, 8 * k:8 * k + 8, :] = total
            for n in range(3):
                geop[n, j, pl.ds(i, CHUNK, stride=tiles), :] = tmp[j, i, pl.ds(8 * (2 * n + 2), CHUNK, stride=2), :]
            return 0
        lax.fori_loop(0, tiles, do, 0)

    def result_moves(j):
        here = span_of(c, j)
        for k in (3, 2, 1, 0):
            gd = lev ^ k
            yield (None if k else (c == l), outp.at[gd, j], out.at[pl.ds(2 * y, 2), here],
                   so.at[j, k], ro.at[j, y], (2 * sb + c, gd))

    def integral_moves(j):
        for n in range(3):
            yield (None if n else (c == 0), geop.at[n, j], above.at[j], sg.at[j, n], rg.at[j], (2 * sb + c, n))

    def send_results(j):
        swap(j).wait_recv()
        remap(j)
        for move in result_moves(j):
            start(*move)

    def send_integrals(*which):
        @pl.when(y == 0)
        def _():
            for j in which:
                integrate(j)
                for move in integral_moves(j):
                    start(*move)

    pass_on(0)
    start_all(courant_moves[2], field_moves[1])
    take_courant(0)

    @pl.when(has_low)
    def _():
        low_row().start()
    take_fields(0)
    send_halo(0)
    pass_on(1)
    zonal(0, [HALO, both - HALO - 1])
    pass_on(2)
    start_all(field_moves[2], thick_moves)

    take_courant(1)
    take_fields(1)
    zonal(0, [first + d for first in both_places(1) for d in range(CHUNK)])

    @pl.when(has_up)
    def _():
        low_row().wait_recv()
    for n, w in enumerate(face_weights(cytop[...])):
        wy[n, :, top:top + 8, :] = w
    wait_halo(0)
    meridional(0, [0, both - 5], 5)
    send_halo(1)
    zonal(1, [3, 4, both - 5, both - 4])

    take_courant(2)
    take_fields(2)
    zonal(0, list(range(8, 16)))
    meridional(0, [5], both - 10)
    zonal(1, list(range(5, 19)))
    wait_halo(1)
    meridional(1, ends, HALO)
    send_halo(2)
    meridional(1, [HALO], both - 2 * HALO)
    zonal(2, list(range(3, 13)))
    zonal(2, list(range(13, 21)))
    meridional(2, [5], both - 10)
    zonal(3, list(range(5, 19)))
    meridional(3, [8], 8)
    send_swap(2)

    take_thickness()
    send_results(2)

    wait_halo(2)
    meridional(2, ends, HALO)
    send_halo(3)
    meridional(2, [HALO, both - 5], 2)
    zonal(3, [3, 4, both - 5, both - 4])
    meridional(3, [HALO, both - 8], 5)
    send_swap(1)
    send_integrals(2)
    send_results(1)

    wait_halo(3)
    meridional(3, ends, HALO)
    send_swap(0)
    send_integrals(1)
    send_results(0)
    send_integrals(0)

    @pl.when(lev < 3)
    def _():
        for j in range(chunks):
            arrived(above.at[j], rg.at[j])

    @pl.when(c == l)
    def _():
        keep_spans.wait()
        give_spans.wait_send()

    @pl.when(c != l)
    def _():
        give_spans.wait_recv()
    for j in range(chunks):
        for s in range(4):
            arrived(out.at[pl.ds(2 * s, 2), span_of(l, j)], ro.at[j, s])

    for group in courant_moves + field_moves + [thick_moves]:
        for move in group:
            sent(*move)
    for j in range(chunks):
        for kind in (1, 2):
            forward(kind, j).wait_send()
    for j in range(chunks):
        swap(j).wait_send()
        for move in result_moves(j):
            sent(*move)

    @pl.when(y == 0)
    def _():
        for j in range(chunks):
            for move in integral_moves(j):
                sent(*move)

    @pl.when(has_low)
    def _():
        low_row().wait_send()
        for t in range(SUBSTEPS):
            to_low(t).wait_send()

    @pl.when(has_up)
    def _():
        for t in range(SUBSTEPS):
            to_up(t).wait_send()


def finish(rows, tiles, result, above, span_in, wts, surface, out, geo, held, over, spans, sgeo, sums, total, sems, gsems):
    lat, lev = lax.axis_index("lat"), lax.axis_index("lev")
    l = lat % 2
    pitch = 2 * tiles
    loads = [pltpu.make_async_copy(above, over, gsems.at[0]), pltpu.make_async_copy(span_in, spans, gsems.at[1]),
             pltpu.make_async_copy(surface, sgeo, gsems.at[2])]
    takes = [pltpu.make_async_copy(result.at[f], held.at[f], sems.at[0, f]) for f in range(8)]
    gives = [pltpu.make_async_copy(held.at[f], out.at[f], sems.at[1, f]) for f in range(8)]
    for copy in takes[:1] + loads + takes[1:]:
        copy.start()
    for take, give in zip(takes, gives):
        take.wait()
        give.start()
    for copy in loads:
        copy.wait()
    for j in range(rows // CHUNK):
        row = jnp.where(l == 0, j * CHUNK, rows - (j + 1) * CHUNK)
        for i in range(tiles):
            sums[pl.ds(row * tiles + i, CHUNK, stride=tiles), :] = over[j, pl.ds(i, CHUNK, stride=tiles), :]
    for r0, n in ((0, 8), (8, rows - 8)):
        shape = (n, LANES)
        whole, below, mine = None, jnp.zeros(shape, jnp.float32), [None, None]
        for k in range(8):
            weight = jnp.full(shape, wts[k], jnp.float32)
            whole = weight if whole is None else whole + weight
            below = below + jnp.where(k < 2 * lev, weight, 0.0)
            mine[k % 2] = weight if k < 2 else jnp.where(k // 2 == lev, weight, mine[k % 2])
        inverse = 1.0 / whole
        shares = [mine[0] * inverse, mine[1] * inverse]
        fractions = [(below + mine[0]) * inverse, (below + mine[0] + mine[1]) * inverse]
        for i in range(tiles):
            span = spans[pl.ds(r0 * tiles + i, n, stride=tiles), :]
            value = jnp.where(lev < 3, sums[pl.ds(r0 * tiles + i, n, stride=tiles), :], 0.0)
            value = value + sgeo[r0:r0 + n, i * LANES:(i + 1) * LANES]
            for a in (1, 0):
                here = pl.ds(r0 * pitch + 2 * i + a, n, stride=pitch)
                low = TOP_PRESSURE + span * fractions[a]
                up = low - span * shares[a]
                value = value + GAS_FACTOR * held[0, here, :] / (low - up) * jnp.log(low / up)
                total[here, :] = value
    store = pltpu.make_async_copy(total, geo, gsems.at[3])
    store.start()
    for copy in gives + [store]:
        copy.wait()


def in_lines(array):
    lead = array.ndim - 3
    levels, rows, nlon = array.shape[lead:]
    tiles = nlon // LANES
    split = array.reshape(array.shape[:-1] + (tiles, LANES))
    order = tuple(range(lead)) + (lead + 1, lead + 2, lead, lead + 3)
    split = with_layout_constraint(split, Layout(major_to_minor=order))
    return jnp.transpose(split, order).reshape(array.shape[:lead] + (rows * tiles * levels, LANES))


def from_lines(array, levels, rows):
    lead = array.ndim - 2
    tiles = array.shape[-2] // (levels * rows)
    split = array.reshape(array.shape[:lead] + (rows, tiles, levels, LANES))
    split = jnp.transpose(split, tuple(range(lead)) + (lead + 2, lead, lead + 1, lead + 3))
    order = tuple(range(lead)) + (lead + 1, lead + 2, lead, lead + 3)
    split = with_layout_constraint(split, Layout(major_to_minor=order))
    return split.reshape(array.shape[:lead] + (levels, rows, tiles * LANES))


def body(nsuper, tracers, courant_x, courant_y, thickness, level_weights, surface_geo):
    levels, rows, nlon = thickness.shape
    tiles = nlon // LANES
    f32 = jnp.float32
    hbm = pl.BlockSpec(memory_space=pltpu.HBM)
    both = 2 * rows
    lines = rows * tiles * levels
    chunks = rows // CHUNK
    sum_lines = -(-CHUNK * tiles // 8) * 8
    span_lines = -(-rows * tiles // 8) * 8

    def buffer(*shape):
        return pltpu.VMEM(shape + (LANES,), f32)

    dma = pltpu.SemaphoreType.DMA
    scratch = [
        pltpu.SMEM((8,), f32), dma, buffer(span_lines),
        buffer(4, 2, lines), buffer(4, lines), buffer(4, lines), buffer(4, lines),
        buffer(SUBSTEPS + 1, tiles, 8 * both), buffer(SUBSTEPS, tiles, 8 * (both + 2 * HALO)),
        buffer(tiles, 8 * both), buffer(tiles, 8 * both),
        buffer(7, tiles, 8 * both), buffer(3, tiles, 8 * (both + 1)),
        buffer(tiles, 8), buffer(tiles, 8), buffer(chunks, tiles, 64),
        buffer(2, chunks, tiles, 8 * CHUNK), buffer(chunks, tiles, 64),
        buffer(4, chunks, 2, lines // chunks), buffer(3, chunks, sum_lines),
        pltpu.VMEM((2 * LANES, len(SHIFTS) * LANES), jnp.bfloat16),
        dma((3, chunks, 4)), dma((3, chunks, 4)), dma((4,)), dma((4,)), dma((SUBSTEPS, 2)), dma((SUBSTEPS, 2)),
        dma, dma, dma((chunks,)), dma((chunks,)),
        dma((chunks, 4)), dma((chunks, 4)), dma((chunks, 3)), dma((chunks,)), dma((3,)), dma((2, chunks)),
    ]
    results = jax.ShapeDtypeStruct((8, lines, LANES), f32)
    result, above, spans = pl.pallas_call(
        functools.partial(kernel, nsuper, rows, tiles),
        out_shape=(results, jax.ShapeDtypeStruct((chunks, sum_lines, LANES), f32),
                   jax.ShapeDtypeStruct((span_lines, LANES), f32)),
        in_specs=[hbm] * 5,
        out_specs=(hbm, hbm, hbm),
        scratch_shapes=scratch,
        compiler_params=pltpu.CompilerParams(
            collective_id=0, has_side_effects=True, vmem_limit_bytes=60 * 2**20),
        name="transport_remap",
    )(in_lines(tracers), in_lines(courant_x), in_lines(courant_y), in_lines(thickness), level_weights)
    out, geo = pl.pallas_call(
        functools.partial(finish, rows, tiles),
        out_shape=(results, jax.ShapeDtypeStruct((lines, LANES), f32)),
        in_specs=[hbm] * 3 + [pl.BlockSpec(memory_space=pltpu.SMEM), hbm],
        out_specs=(hbm, hbm),
        scratch_shapes=[buffer(8, lines), buffer(chunks, sum_lines), buffer(span_lines), pltpu.VMEM((rows, nlon), f32),
                        buffer(span_lines), buffer(lines), dma((2, 8)), dma((4,))],
        compiler_params=pltpu.CompilerParams(vmem_limit_bytes=60 * 2**20),
        name="finish",
    )(result, above, spans, level_weights, surface_geo)
    return from_lines(out, levels, rows), from_lines(geo, levels, rows)


def solution(mesh):
    in_specs = (
        P(None, "lev", "lat", None),
        P("lev", "lat", None),
        P("lev", "lat", None),
        P("lev", "lat", None),
        P(),
        P("lat", None),
    )
    out_specs = (P(None, "lev", "lat", None), P("lev", "lat", None))
    run = functools.partial(body, mesh.shape["lat"] // 2)
    return jax.shard_map(run, mesh=mesh, in_specs=in_specs, out_specs=out_specs, check_vma=False)
```
